256 devices in a mesh: dp: 4 (over x), expert: 64 (over z, y, core).
Axes of the slice: x: 4, y: 4, z: 8, core: 2. Of those that a mesh axis runs over, the one named last changes fastest.
Arguments:
- grad_parts: bfloat16 [4, 256, 192, 2048], P('dp', 'expert'), may hold values from -4 to 4
- old_m_codes: bfloat16 [4, 64, 576, 2048], P('dp', 'expert'), may hold values from -1 to 1
- old_v_codes: bfloat16 [4, 64, 576, 2048], P('dp', 'expert'), may hold values from 0.049804688 to 1
- old_m_scale: bfloat16 [4, 64, 576, 16], P('dp', 'expert'), may hold values from 0.049804688 to 1
- old_v_scale: bfloat16 [4, 64, 576, 16], P('dp', 'expert'), may hold values from 0.049804688 to 1
- expert_map: int32 [256], replicated, may hold values from 0 to 255, as said below
- slot_expert: int32 [64, 576], P('expert'), may hold values from 0 to 255, as said below
- slot_row: int32 [64, 576], P('expert'), may hold values from 0 to 47
- peer_count: int32 [64, 64], P('expert'), may hold values from 0 to 9, as said below
- peer_offset: int32 [64, 64], P('expert'), may hold values from 0 to 567, as said below
Outputs:
- direction: float32 [256, 192, 2048], P('expert', 'dp')
- new_codes: bfloat16 [2, 256, 192, 2048], P(None, 'expert', 'dp')
- new_scales: bfloat16 [2, 256, 192, 16], P(None, 'expert', 'dp')
The draws below stay inside these ranges and needn't reach their ends.
Inputs may be any that keep to these rules, and one draw needn't show every extreme that they name: expert_map is a permutation. `slot_expert`: each row of the new layout, on each dp index, is held by exactly one live slot; slots past a reader's load hold 0. `peer_count`: A reader's slots are ordered by owner; each owner receives 192 rows in all; some reader holds 9 slots for every owner, and 4 readers hold none. peer_offset is the running total of peer_count over owners before each.
All inputs are finite; a program needn't handle non-finite values. Where the reference program divides by a largest or mean magnitude, that divisor is 1e-20 or more.
Results may differ from the reference program's by a relative error of at most 0.018.
Values may be sent and summed in bfloat16 or wider, within the bound.
A program may use at most 128 MiB of HBM per device.

```python
import math
import jax
import jax.numpy as jnp
from jax import lax

H = 2048
EXP_DEV = 4
QB = 128
ROWS = 192
EXPERTS = 256
RDP = 48
PPD = 192
CAP = 576
PEER_MOST = 9
HB = 16
LOST = 4
N_DP = 4
N_EXPERT = 64


def reading_plan(key):
    key_map, key_roles, key_shift, key_order = jax.random.split(key, 4)
    expert_map = jax.random.permutation(key_map, EXPERTS).astype(jnp.int32)
    old_of_new = jnp.zeros((EXPERTS,), jnp.int32).at[expert_map].set(jnp.arange(EXPERTS, dtype=jnp.int32))
    reader_roles = jax.random.permutation(key_roles, N_EXPERT).astype(jnp.int32)
    busiest = reader_roles[0]
    active_total = N_EXPERT - 1 - LOST
    active_ids = reader_roles[1 + LOST:]
    shifts = jax.random.randint(key_shift, (N_EXPERT,), 0, active_total).astype(jnp.int32)
    orders = jax.vmap(lambda single: jax.random.permutation(single, PPD))(jax.random.split(key_order, N_EXPERT)).astype(jnp.int32)
    owner_ids = jnp.broadcast_to(jnp.arange(N_EXPERT, dtype=jnp.int32)[:, None], (N_EXPERT, PPD))
    rank_all = jnp.broadcast_to(jnp.arange(PPD, dtype=jnp.int32)[None, :], (N_EXPERT, PPD))
    is_busiest = rank_all < PEER_MOST
    beyond = jnp.maximum(rank_all - PEER_MOST, 0)
    reader_ids = jnp.where(is_busiest, busiest, active_ids[(shifts[:, None] + beyond) % active_total])
    slot_rank = jnp.where(is_busiest, rank_all, beyond // active_total)
    send_counts = jnp.zeros((N_EXPERT, N_EXPERT), jnp.int32).at[reader_ids.reshape(-1), owner_ids.reshape(-1)].add(1)
    offsets = jnp.cumsum(send_counts, axis=1) - send_counts
    position = offsets[reader_ids, owner_ids] + slot_rank
    new_expert = owner_ids * EXP_DEV + orders // RDP
    expert_ids = jnp.zeros((N_EXPERT, CAP), jnp.int32).at[reader_ids, position].set(old_of_new[new_expert])
    row_ids = jnp.zeros((N_EXPERT, CAP), jnp.int32).at[reader_ids, position].set(orders % RDP)
    return (expert_map, expert_ids, row_ids, send_counts, offsets)


def draw_expert_map(key, part):
    return reading_plan(key)[0]


def draw_slot_expert(key, part):
    return reading_plan(key)[1]


def draw_slot_row(key, part):
    return reading_plan(key)[2]


def draw_peer_count(key, part):
    return reading_plan(key)[3]


def draw_peer_offset(key, part):
    return reading_plan(key)[4]


def levels(rng, extent, shards, smallest, high):
    loudness, own = 1.0, jax.random.fold_in(rng, 6)
    for dim, parts in shards:
        draws = jnp.exp(jax.random.uniform(jax.random.fold_in(own, dim), (parts,), jnp.float32, smallest / len(shards), high / len(shards)))
        loudness = loudness * jnp.repeat(draws, extent[dim] // parts).reshape([-1 if axis == dim else 1 for axis in range(len(extent))])
    return loudness


def bell_draw(rng, shape, deviation, bound, shards=(), kind=jnp.bfloat16):
    array = jax.random.normal(rng, shape, jnp.float32) * deviation
    if len(shards) > 0:
        array = levels(rng, shape, shards, -0.22, 0.18) * array
    return jnp.clip(array, min=-bound, max=bound).astype(kind)


def setup_inputs(seed: int = 0) -> dict:
    splits = jax.random.split(jax.random.key(seed), 11)
    return {
        "grad_parts": bell_draw(splits[0], (N_DP, EXPERTS, ROWS, H), 0.5, 4.0, ((0, 4), (1, 64))),
        "old_m_codes": jnp.clip(jax.random.uniform(splits[1], (N_DP, N_EXPERT, CAP, H), jnp.float32, -1.0, 1.0) * levels(splits[1], (N_DP, N_EXPERT, CAP, H), ((0, 4), (1, 64)), -0.4, 0.0), -1.0, 1.0).astype(jnp.bfloat16),
        "old_v_codes": jnp.clip(0.049804688 + 0.9501953 * jax.random.uniform(splits[2], (N_DP, N_EXPERT, CAP, H), jnp.float32) ** levels(splits[2], (N_DP, N_EXPERT, CAP, H), ((0, 4), (1, 64)), -0.2, 0.2), 0.049804688, 1.0).astype(jnp.bfloat16),
        "old_m_scale": jnp.clip(jnp.exp(math.log(1.0) - 2.9996462 * jax.random.uniform(splits[3], (N_DP, N_EXPERT, CAP, HB), jnp.float32) ** levels(splits[3], (N_DP, N_EXPERT, CAP, HB), ((0, 4), (1, 64)), -0.2, 0.2)), 0.049804688, 1.0).astype(jnp.bfloat16),
        "old_v_scale": jnp.clip(jnp.exp(math.log(1.0) - 2.9996462 * jax.random.uniform(splits[4], (N_DP, N_EXPERT, CAP, HB), jnp.float32) ** levels(splits[4], (N_DP, N_EXPERT, CAP, HB), ((0, 4), (1, 64)), -0.2, 0.2)), 0.049804688, 1.0).astype(jnp.bfloat16),
        "expert_map": draw_expert_map(jax.random.fold_in(splits[10], 71), 0),
        "slot_expert": draw_slot_expert(jax.random.fold_in(splits[10], 71), 0),
        "slot_row": draw_slot_row(jax.random.fold_in(splits[10], 71), 0),
        "peer_count": draw_peer_count(jax.random.fold_in(splits[10], 71), 0),
        "peer_offset": draw_peer_offset(jax.random.fold_in(splits[10], 71), 0),
    }


beta_one = 0.9
beta_two = 0.95
adam_eps = 1e-08
scale_eps = 1e-06

def dequantize(code_array, block_scale):
    full_shape = code_array.shape
    blocks = code_array.astype(jnp.float32).reshape(full_shape[:-1] + (full_shape[-1] // QB, QB))
    return (blocks * block_scale.astype(jnp.float32)[..., None]).reshape(full_shape)

def quantize(values):
    full_shape = values.shape
    blocks = values.reshape(full_shape[:-1] + (full_shape[-1] // QB, QB))
    block_scale = (lax.optimization_barrier(jnp.max(jnp.abs(blocks), axis=-1)) + scale_eps).astype(jnp.bfloat16)
    code_array = (blocks / block_scale.astype(jnp.float32)[..., None]).astype(jnp.bfloat16)
    return (code_array.reshape(full_shape), block_scale)

def reference(grad_parts, old_m_codes, old_v_codes, old_m_scale, old_v_scale, expert_map, slot_expert, slot_row, peer_count, peer_offset):
    owner_rows = EXPERTS * RDP
    target_expert = expert_map[slot_expert]
    dest_owner = target_expert // EXP_DEV
    place = jnp.arange(CAP, dtype=jnp.int32)[None, :] - jnp.take_along_axis(peer_offset, dest_owner, axis=1)
    usable = (place >= 0) & (place < jnp.take_along_axis(peer_count, dest_owner, axis=1))
    target = jnp.where(usable, target_expert * RDP + slot_row, owner_rows).reshape(-1)
    grad_total = lax.optimization_barrier(jnp.sum(grad_parts.astype(jnp.float32), axis=0))
    direction_parts, m_codes, v_codes, m_scales, v_scales = ([], [], [], [], [])
    for replica in range(N_DP):
        first_old = dequantize(old_m_codes[replica], old_m_scale[replica]).reshape(N_EXPERT * CAP, H)
        second_old = dequantize(old_v_codes[replica], old_v_scale[replica]).reshape(N_EXPERT * CAP, H)
        first_moment = jnp.zeros((owner_rows, H), jnp.float32).at[target].set(first_old, mode='drop').reshape(EXPERTS, RDP, H)
        second_moment = jnp.zeros((owner_rows, H), jnp.float32).at[target].set(second_old, mode='drop').reshape(EXPERTS, RDP, H)
        grad_share = grad_total[:, replica * RDP:(replica + 1) * RDP]
        first_new = beta_one * first_moment + (1.0 - beta_one) * grad_share
        second_new = beta_two * second_moment + (1.0 - beta_two) * grad_share * grad_share
        direction_parts.append(first_new / (jnp.sqrt(second_new) + adam_eps))
        code_first, scale_first = quantize(first_new)
        code_second, scale_second = quantize(second_new)
        m_codes.append(code_first)
        v_codes.append(code_second)
        m_scales.append(scale_first)
        v_scales.append(scale_second)
    direction = jnp.concatenate(direction_parts, axis=1)
    new_codes = jnp.stack([jnp.concatenate(m_codes, axis=1), jnp.concatenate(v_codes, axis=1)])
    new_scales = jnp.stack([jnp.concatenate(m_scales, axis=1), jnp.concatenate(v_scales, axis=1)])
    return (direction, new_codes, new_scales)
```

```python
import functools

import jax
import jax.numpy as jnp
from jax import lax
from jax.experimental import pallas as pl
from jax.experimental.pallas import tpu as pltpu
from jax.sharding import PartitionSpec as P

beta_one = 0.9
beta_two = 0.95
adam_eps = 1e-08
scale_eps = 1e-06

MESH = pl.DeviceIdType.MESH
f32 = jnp.float32
bf16 = jnp.bfloat16
BASE = 4
EXTRA = 5


def dequantize(code_array, block_scale):
    full_shape = code_array.shape
    blocks = code_array.astype(jnp.float32).reshape(
        full_shape[:-1] + (block_scale.shape[-1], full_shape[-1] // block_scale.shape[-1])
    )
    return (blocks * block_scale.astype(jnp.float32)[..., None]).reshape(full_shape)


def quantize(values, block_count):
    full_shape = values.shape
    blocks = values.reshape(full_shape[:-1] + (block_count, full_shape[-1] // block_count))
    block_scale = (jnp.max(jnp.abs(blocks), axis=-1) + scale_eps).astype(jnp.bfloat16)
    code_array = (blocks / block_scale.astype(jnp.float32)[..., None]).astype(jnp.bfloat16)
    return (code_array.reshape(full_shape), block_scale)


def padded_exchange(
    grad_parts,
    old_m_codes,
    old_v_codes,
    old_m_scale,
    old_v_scale,
    expert_map,
    slot_expert,
    slot_row,
    peer_count,
    peer_offset,
):
    owners = lax.axis_size("expert")
    codes_first = old_m_codes[0, 0]
    codes_second = old_v_codes[0, 0]
    scale_first = old_m_scale[0, 0]
    scale_second = old_v_scale[0, 0]
    slot_total = codes_first.shape[0]
    width = codes_first.shape[1]
    block_count = scale_first.shape[1]
    per_peer = slot_total // owners
    exp_dev = grad_parts.shape[1]
    share_rows = grad_parts.shape[2] // lax.axis_size("dp")
    owned_rows = exp_dev * share_rows
    send_counts = peer_count[0]
    offsets = peer_offset[0]
    slot_place = jnp.arange(per_peer, dtype=jnp.int32)[None, :]
    picked = (offsets[:, None] + slot_place).reshape(-1)
    new_expert = expert_map[slot_expert[0]]
    local_all = new_expert % exp_dev * share_rows + slot_row[0]
    usable = slot_place < send_counts[:, None]
    targets = jnp.where(usable, local_all[picked].reshape(owners, per_peer), -1)
    arrived_targets = lax.all_to_all(targets, "expert", split_axis=0, concat_axis=0, tiled=True)
    sent_first = dequantize(codes_first[picked], scale_first[picked]).reshape(
        owners, per_peer, width
    )
    sent_second = dequantize(codes_second[picked], scale_second[picked]).reshape(
        owners, per_peer, width
    )
    first_rows = lax.all_to_all(
        sent_first.astype(jnp.bfloat16), "expert", split_axis=0, concat_axis=0, tiled=True
    ).astype(sent_first.dtype)
    second_rows = lax.all_to_all(
        sent_second.astype(jnp.bfloat16), "expert", split_axis=0, concat_axis=0, tiled=True
    ).astype(sent_second.dtype)
    flat_targets = arrived_targets.reshape(-1)
    landing = jnp.where(flat_targets >= 0, flat_targets, owned_rows)
    first_moment = (
        jnp.zeros((owned_rows, width), jnp.float32)
        .at[landing]
        .set(first_rows.reshape(-1, width), mode="drop")
    )
    second_moment = (
        jnp.zeros((owned_rows, width), jnp.float32)
        .at[landing]
        .set(second_rows.reshape(-1, width), mode="drop")
    )
    first_moment, second_moment = (
        first_moment.reshape(exp_dev, share_rows, width),
        second_moment.reshape(exp_dev, share_rows, width),
    )
    grad_share = lax.psum_scatter(grad_parts[0], "dp", scatter_dimension=1, tiled=True).astype(
        jnp.float32
    )
    first_new = beta_one * first_moment + (1.0 - beta_one) * grad_share
    second_new = beta_two * second_moment + (1.0 - beta_two) * grad_share * grad_share
    direction = first_new / (jnp.sqrt(second_new) + adam_eps)
    code_first, new_scale_first = quantize(first_new, block_count)
    code_second, new_scale_second = quantize(second_new, block_count)
    return (
        direction,
        jnp.stack([code_first, code_second]),
        jnp.stack([new_scale_first, new_scale_second]),
    )


def iota(shape, dim):
    return lax.broadcasted_iota(jnp.int32, shape, dim)


def dot(a, b, dims=((1,), (0,))):
    return lax.dot_general(a, b, (dims, ((), ())), preferred_element_type=f32)


def pick(rows, chosen, vector):
    return jnp.sum(jnp.where(chosen, vector, 0.0), axis=1, keepdims=True)


def resume_kernel(
    grad_ref,
    m_ref,
    v_ref,
    ms_ref,
    vs_ref,
    map_ref,
    expert_ref,
    row_ref,
    count_ref,
    offset_ref,
    dir_ref,
    codes_ref,
    scales_ref,
    flag_ref,
    moments,
    relay,
    extra,
    extra_core,
    extra_y,
    extra_z,
    part_core,
    part_y,
    send,
    recv,
    meta_send,
    meta_recv,
    grads,
    place,
    late,
    landed,
    send_sem,
    recv_sem,
    meta_ssem,
    meta_rsem,
    grad_ssem,
    grad_rsem,
    core_sem,
    y_ssem,
    y_rsem,
    z_ssem,
    z_rsem,
):
    d = lax.axis_index("dp")
    e = lax.axis_index("expert")
    z, y, k = lax.div(e, 8), lax.rem(lax.div(e, 2), 4), lax.rem(e, 2)
    share = grads.shape[2]

    def peer(i):
        pz = lax.rem(z + lax.div(i, 8), 8)
        py = lax.rem(y + lax.rem(lax.div(i, 2), 4), 4)
        pk = lax.rem(k + lax.rem(i, 2), 2)
        return pz * 8 + py * 2 + pk

    barrier = pltpu.get_barrier_semaphore()

    def greet(i, carry):
        pl.semaphore_signal(barrier, inc=1, device_id=(d, peer(i)), device_id_type=MESH)
        return carry

    lax.fori_loop(1, 64, greet, 0)
    for dx in range(1, 4):
        pl.semaphore_signal(
            barrier, inc=1, device_id=(lax.rem(d + dx, 4), e), device_id_type=MESH
        )

    for b in range(16):
        lanes = slice(b * 128, (b + 1) * 128)
        moments[:, b * 128 : (b + 1) * 128] = (
            m_ref[:, lanes].astype(f32) * ms_ref[:, b : b + 1].astype(f32)
        ).astype(bf16)
        moments[:, 2048 + b * 128 : 2048 + (b + 1) * 128] = (
            v_ref[:, lanes].astype(f32) * vs_ref[:, b : b + 1].astype(f32)
        ).astype(bf16)

    count = count_ref[...].astype(f32)
    offset = offset_ref[...].astype(f32)
    slots = m_ref.shape[0]

    row, col = iota((64 * EXTRA, 64), 0), iota((64 * EXTRA, 64), 1)
    u = row & 63
    owner = ((u & 7) << 3) | (((u >> 3) & 3) << 1) | (u >> 5)
    chosen = owner == col
    s = (iota((64 * EXTRA, 1), 0) >> 6).astype(f32) + float(BASE)
    source = jnp.where(
        s < pick(64 * EXTRA, chosen, count), pick(64 * EXTRA, chosen, offset) + s, -1.0
    )
    slot_lane = iota((64 * EXTRA, slots), 1).astype(f32)
    take_extra = (slot_lane == source).astype(bf16)
    for c in range(8):
        rows = dot(take_extra, moments[:, c * 512 : (c + 1) * 512])
        for s_i in range(EXTRA):
            for q in range(4):
                relay[pl.ds(s_i * 32 + c * 4 + q, 64, stride=32 * EXTRA), :] = rows[
                    s_i * 64 : (s_i + 1) * 64, q * 128 : (q + 1) * 128
                ]

    def narrow(u, carry):
        extra[u] = relay[pl.ds(pl.multiple_of(u * 32 * EXTRA, 32), 32 * EXTRA), :].astype(bf16)
        return carry

    lax.fori_loop(0, 64, narrow, 0)

    orow, ocol = iota((64, 64), 0), iota((64, 64), 1)
    count_col = pick(64, orow == ocol, count)
    offset_col = pick(64, orow == ocol, offset)
    lane = iota((64, slots), 1).astype(f32)
    held = jnp.logical_and(lane >= offset_col, lane < offset_col + count_col)
    rank = iota((1, slots), 1).astype(f32) - jnp.sum(
        jnp.where(held, offset_col, 0.0), axis=0, keepdims=True
    )
    old = iota((256, slots), 0) == expert_ref[...]
    mapped = dot(
        jnp.broadcast_to(map_ref[...].astype(f32), (8, 256)).astype(bf16), old.astype(bf16)
    )[0:1]
    land = (mapped - 4.0 * jnp.floor(mapped * 0.25)) * float(share) + row_ref[...].astype(f32) + 1.0
    held_land = jnp.where(held, land, 0.0).astype(bf16)
    at_rank = (iota((128, slots), 0).astype(f32) == rank).astype(bf16)
    targets = dot(held_land, at_rank, ((1,), (1,)))
    shift = (iota((64, 128), 0) + 64 == iota((64, 128), 1)).astype(bf16)
    counts = dot(jnp.broadcast_to(count, (64, 64)).astype(bf16), shift)
    meta_send[...] = jnp.where(iota((64, 128), 1) < 16, targets, counts)

    pl.semaphore_wait(barrier, 66)

    def grad_copy(dx):
        to = lax.rem(d + dx, 4)
        return pltpu.make_async_remote_copy(
            src_ref=grad_ref.at[0, :, pl.ds(pl.multiple_of(to * share, 16), share), :],
            dst_ref=grads.at[dx],
            send_sem=grad_ssem.at[dx],
            recv_sem=grad_rsem.at[dx],
            device_id=(to, e),
            device_id_type=MESH,
        )

    own_grad = pltpu.make_async_copy(
        grad_ref.at[0, :, pl.ds(pl.multiple_of(d * share, 16), share), :], grads.at[0], grad_ssem.at[0]
    )
    for dx in range(1, 4):
        grad_copy(dx).start()
    own_grad.start()

    core_copy = pltpu.make_async_remote_copy(
        src_ref=extra.at[pl.ds((1 - k) * 32, 32)],
        dst_ref=extra_core,
        send_sem=core_sem.at[0],
        recv_sem=core_sem.at[1],
        device_id=(d, peer(1)),
        device_id_type=MESH,
    )
    core_copy.start()

    def meta_copy(i):
        to = peer(i)
        return pltpu.make_async_remote_copy(
            src_ref=meta_send.at[pl.ds(to, 1)],
            dst_ref=meta_recv.at[pl.ds(i, 1)],
            send_sem=meta_ssem.at[i],
            recv_sem=meta_rsem.at[i],
            device_id=(d, to),
            device_id_type=MESH,
        )

    def main_copy(i):
        to = peer(i)
        return pltpu.make_async_remote_copy(
            src_ref=send.at[to],
            dst_ref=recv.at[i],
            send_sem=send_sem.at[i],
            recv_sem=recv_sem.at[i],
            device_id=(d, to),
            device_id_type=MESH,
        )

    def start_meta(i, carry):
        meta_copy(i).start()
        return carry

    def start_main(i, carry):
        main_copy(i).start()
        return carry

    row, col = iota((512, 64), 0), iota((512, 64), 1)
    chosen = (row >> 3) == col
    s = (iota((512, 1), 0) & 3).astype(f32)
    source = jnp.where(s < pick(512, chosen, count), pick(512, chosen, offset) + s, -1.0)
    take = (iota((512, slots), 1).astype(f32) == source).astype(bf16)
    low = (iota((512, 256), 0) & 7) < 4
    for c in range(4):
        quarter = [
            dot(take, moments[:, q * 1024 + c * 256 : q * 1024 + (c + 1) * 256]) for q in range(4)
        ]
        upper = jnp.where(low, quarter[0], quarter[1]).reshape(64, 8, 256)
        lower = jnp.where(low, quarter[2], quarter[3]).reshape(64, 8, 256)
        send[:, :, c * 256 : (c + 1) * 256] = jnp.concatenate([upper, lower], axis=1).astype(bf16)

    core_copy.wait()
    mine = pl.ds(k * 32, 32)

    def add_core(g, carry):
        part_core[g] = extra[k * 32 + g] + extra_core[g]
        return carry

    lax.fori_loop(0, 32, add_core, 0)

    def y_copy(dy):
        to = lax.rem(y + dy, 4)
        return pltpu.make_async_remote_copy(
            src_ref=part_core.at[pl.ds(to * 8, 8)],
            dst_ref=extra_y.at[dy - 1],
            send_sem=y_ssem.at[dy - 1],
            recv_sem=y_rsem.at[dy - 1],
            device_id=(d, z * 8 + to * 2 + k),
            device_id_type=MESH,
        )

    def z_copy(dz):
        to = lax.rem(z + dz, 8)
        return pltpu.make_async_remote_copy(
            src_ref=part_y.at[to],
            dst_ref=extra_z.at[dz - 1],
            send_sem=z_ssem.at[dz - 1],
            recv_sem=z_rsem.at[dz - 1],
            device_id=(d, to * 8 + y * 2 + k),
            device_id_type=MESH,
        )

    for dy in range(1, 4):
        y_copy(dy).start()
    lax.fori_loop(24, 48, start_main, 0)
    for dy in range(1, 4):
        y_copy(dy).wait()

    def add_y(g, carry):
        part_y[g] = part_core[y * 8 + g] + (extra_y[0, g] + (extra_y[1, g] + extra_y[2, g]))
        return carry

    lax.fori_loop(0, 8, add_y, 0)
    for dz in range(1, 8):
        z_copy(dz).start()
    lax.fori_loop(48, 64, start_main, 0)
    lax.fori_loop(1, 24, start_main, 0)
    lax.fori_loop(1, 64, start_meta, 0)

    recv[0] = send[e]
    meta_recv[pl.ds(0, 1), :] = meta_send[pl.ds(e, 1), :]

    def wait_meta(i, carry):
        meta_copy(i).wait()
        return carry

    lax.fori_loop(1, 64, wait_meta, 0)
    meta = meta_recv[...]

    heavy = jnp.sum((meta > float(BASE)).astype(f32), axis=0, keepdims=True)
    heavy = jnp.where(iota((1, 128), 1) >= 64, heavy, 0.0)
    flag_ref[...] = jnp.broadcast_to(jnp.max(heavy, axis=1, keepdims=True), (8, 128))

    spread = (iota((64, 1024), 0) == (iota((64, 1024), 1) >> 4)).astype(bf16)
    by_slot = dot(meta.astype(bf16), spread, ((0,), (0,)))[0:8]
    lane = iota((1, 1024), 1)
    goal = jnp.sum(
        jnp.where(iota((8, 1024), 0) == (lane & 3), by_slot, 0.0), axis=0, keepdims=True
    )
    owned = 4 * share
    hit = iota((owned, 1024), 0).astype(f32) + 1.0 == goal
    for q in range(4):
        place[q * owned : (q + 1) * owned, :] = jnp.where(
            jnp.logical_and(hit, ((lane >> 2) & 3) == q), 1.0, 0.0
        ).astype(bf16)
    late_goal = jnp.sum(meta, axis=0, keepdims=True)
    late_lane = iota((owned, 128), 1)
    late_hit = jnp.logical_and(
        iota((owned, 128), 0).astype(f32) + 1.0 == late_goal,
        jnp.logical_and(late_lane >= BASE, late_lane < BASE + EXTRA),
    )
    late_place = jnp.where(late_hit, 1.0, 0.0).astype(bf16)[:, :16]

    for dz in range(1, 8):
        z_copy(dz).wait()
    late[...] = jnp.zeros_like(late)
    total = part_y[z].astype(f32)
    for dz in range(1, 8):
        total = total + extra_z[dz - 1].astype(f32)
    late[BASE * 32 : (BASE + EXTRA) * 32, :] = total

    def wait_main(i, carry):
        main_copy(i).wait()
        return carry

    lax.fori_loop(1, 64, wait_main, 0)
    own_grad.wait()
    for dx in range(1, 4):
        grad_copy(dx).wait()

    for c in range(4):
        lanes = slice(c * 256, (c + 1) * 256)
        arrived = dot(place[...], recv[:, :, lanes].reshape(1024, 256))
        for q in range(4):
            block = q * 8 + c * 2
            rest = jnp.concatenate(
                [late[pl.ds(block, 16, stride=32), :], late[pl.ds(block + 1, 16, stride=32), :]], axis=1
            ).astype(bf16)
            landed[q * owned : (q + 1) * owned, lanes] = arrived[q * owned : (q + 1) * owned] + dot(
                late_place, rest
            )

    def update(ex, carry):
        scale_lane = iota((share, 16), 1)
        m_scales = jnp.zeros((share, 16), f32)
        v_scales = jnp.zeros((share, 16), f32)
        for b in range(16):
            at = pl.ds(pl.multiple_of(ex * share + (b // 8) * owned, 16), share)
            at_v = pl.ds(pl.multiple_of(ex * share + (2 + b // 8) * owned, 16), share)
            lanes = slice((b % 8) * 128, (b % 8 + 1) * 128)
            out = slice(b * 128, (b + 1) * 128)
            g = (grads[0, ex, :, out].astype(f32) + grads[1, ex, :, out].astype(f32)) + (
                grads[2, ex, :, out].astype(f32) + grads[3, ex, :, out].astype(f32)
            )
            m = beta_one * landed[at, lanes] + (1.0 - beta_one) * g
            v = beta_two * landed[at_v, lanes] + (1.0 - beta_two) * g * g
            dir_ref[ex, :, out] = m / (jnp.sqrt(v) + adam_eps)
            m_scale = (jnp.max(jnp.abs(m), axis=1, keepdims=True) + scale_eps).astype(bf16)
            v_scale = (jnp.max(jnp.abs(v), axis=1, keepdims=True) + scale_eps).astype(bf16)
            m_wide, v_wide = m_scale.astype(f32), v_scale.astype(f32)
            codes_ref[0, ex, :, out] = (m * (1.0 / m_wide)).astype(bf16)
            codes_ref[1, ex, :, out] = (v * (1.0 / v_wide)).astype(bf16)
            m_scales = jnp.where(scale_lane == b, m_wide, m_scales)
            v_scales = jnp.where(scale_lane == b, v_wide, v_scales)
        scales_ref[0, ex] = m_scales.astype(bf16)
        scales_ref[1, ex] = v_scales.astype(bf16)
        return carry

    lax.fori_loop(0, 4, update, 0)


def exchange(grad_parts, m_codes, v_codes, m_scale, v_scale, expert_map, slot_expert, slot_row, count, offset):
    slots, width, blocks = m_codes.shape[2], m_codes.shape[3], m_scale.shape[3]
    share = grad_parts.shape[2] // 4
    owned = 4 * share
    vmem = pl.BlockSpec(memory_space=pltpu.VMEM)
    chunk = 32 * EXTRA
    return pl.pallas_call(
        resume_kernel,
        out_shape=(
            jax.ShapeDtypeStruct((4, share, width), f32),
            jax.ShapeDtypeStruct((2, 4, share, width), bf16),
            jax.ShapeDtypeStruct((2, 4, share, blocks), bf16),
            jax.ShapeDtypeStruct((8, 128), f32),
        ),
        in_specs=[pl.BlockSpec(memory_space=pl.ANY)] + [vmem] * 9,
        out_specs=(vmem,) * 4,
        scratch_shapes=[
            pltpu.VMEM((slots, 2 * width), bf16),
            pltpu.VMEM((64 * chunk, 128), f32),
            pltpu.VMEM((64, chunk, 128), bf16),
            pltpu.VMEM((32, chunk, 128), bf16),
            pltpu.VMEM((3, 8, chunk, 128), bf16),
            pltpu.VMEM((7, chunk, 128), bf16),
            pltpu.VMEM((32, chunk, 128), bf16),
            pltpu.VMEM((8, chunk, 128), bf16),
            pltpu.VMEM((64, 16, 1024), bf16),
            pltpu.VMEM((64, 16, 1024), bf16),
            pltpu.VMEM((64, 128), f32),
            pltpu.VMEM((64, 128), f32),
            pltpu.VMEM((4, 4, share, width), bf16),
            pltpu.VMEM((4 * owned, 1024), bf16),
            pltpu.VMEM((16 * 32, 128), f32),
            pltpu.VMEM((4 * owned, 1024), f32),
            pltpu.SemaphoreType.DMA((64,)),
            pltpu.SemaphoreType.DMA((64,)),
            pltpu.SemaphoreType.DMA((64,)),
            pltpu.SemaphoreType.DMA((64,)),
            pltpu.SemaphoreType.DMA((4,)),
            pltpu.SemaphoreType.DMA((4,)),
            pltpu.SemaphoreType.DMA((2,)),
            pltpu.SemaphoreType.DMA((3,)),
            pltpu.SemaphoreType.DMA((3,)),
            pltpu.SemaphoreType.DMA((7,)),
            pltpu.SemaphoreType.DMA((7,)),
        ],
        compiler_params=pltpu.CompilerParams(
            collective_id=0, has_side_effects=True, vmem_limit_bytes=56 * 2**20
        ),
        name="resume",
    )(
        grad_parts,
        m_codes[0, 0],
        v_codes[0, 0],
        m_scale[0, 0],
        v_scale[0, 0],
        expert_map.reshape(1, -1),
        slot_expert,
        slot_row,
        count,
        offset,
    )


def per_device(*args):
    direction, codes, scales, heavy = exchange(*args)
    return lax.cond(
        heavy[0, 0] < 1.5,
        lambda: (direction, codes, scales),
        lambda: padded_exchange(*args),
    )


def solution(mesh):
    in_specs = (
        P("dp", "expert", None, None),
        P("dp", "expert", None, None),
        P("dp", "expert", None, None),
        P("dp", "expert", None, None),
        P("dp", "expert", None, None),
        P(),
        P("expert", None),
        P("expert", None),
        P("expert", None),
        P("expert", None),
    )
    out_specs = (
        P("expert", "dp", None),
        P(None, "expert", "dp", None),
        P(None, "expert", "dp", None),
    )
    return jax.shard_map(
        per_device, mesh=mesh, in_specs=in_specs, out_specs=out_specs, check_vma=False
    )
```

```python
import functools

import jax
import jax.numpy as jnp
from jax import lax
from jax.experimental import pallas as pl
from jax.experimental.pallas import tpu as pltpu
from jax.sharding import PartitionSpec as P

beta_one = 0.9
beta_two = 0.95
adam_eps = 1e-08
scale_eps = 1e-06

MESH = pl.DeviceIdType.MESH
f32 = jnp.float32
bf16 = jnp.bfloat16
BASE = 4
EXTRA = 5
VMEM_MIB = 44


def dequantize(code_array, block_scale):
    full_shape = code_array.shape
    blocks = code_array.astype(jnp.float32).reshape(
        full_shape[:-1] + (block_scale.shape[-1], full_shape[-1] // block_scale.shape[-1])
    )
    return (blocks * block_scale.astype(jnp.float32)[..., None]).reshape(full_shape)


def quantize(values, block_count):
    full_shape = values.shape
    blocks = values.reshape(full_shape[:-1] + (block_count, full_shape[-1] // block_count))
    block_scale = (jnp.max(jnp.abs(blocks), axis=-1) + scale_eps).astype(jnp.bfloat16)
    code_array = (blocks / block_scale.astype(jnp.float32)[..., None]).astype(jnp.bfloat16)
    return (code_array.reshape(full_shape), block_scale)


def padded_exchange(
    grad_parts,
    old_m_codes,
    old_v_codes,
    old_m_scale,
    old_v_scale,
    expert_map,
    slot_expert,
    slot_row,
    peer_count,
    peer_offset,
):
    owners = lax.axis_size("expert")
    codes_first = old_m_codes[0, 0]
    codes_second = old_v_codes[0, 0]
    scale_first = old_m_scale[0, 0]
    scale_second = old_v_scale[0, 0]
    slot_total = codes_first.shape[0]
    width = codes_first.shape[1]
    block_count = scale_first.shape[1]
    per_peer = slot_total // owners
    exp_dev = grad_parts.shape[1]
    share_rows = grad_parts.shape[2] // lax.axis_size("dp")
    owned_rows = exp_dev * share_rows
    send_counts = peer_count[0]
    offsets = peer_offset[0]
    slot_place = jnp.arange(per_peer, dtype=jnp.int32)[None, :]
    picked = (offsets[:, None] + slot_place).reshape(-1)
    new_expert = expert_map[slot_expert[0]]
    local_all = new_expert % exp_dev * share_rows + slot_row[0]
    usable = slot_place < send_counts[:, None]
    targets = jnp.where(usable, local_all[picked].reshape(owners, per_peer), -1)
    arrived_targets = lax.all_to_all(targets, "expert", split_axis=0, concat_axis=0, tiled=True)
    sent_first = dequantize(codes_first[picked], scale_first[picked]).reshape(
        owners, per_peer, width
    )
    sent_second = dequantize(codes_second[picked], scale_second[picked]).reshape(
        owners, per_peer, width
    )
    first_rows = lax.all_to_all(
        sent_first.astype(jnp.bfloat16), "expert", split_axis=0, concat_axis=0, tiled=True
    ).astype(sent_first.dtype)
    second_rows = lax.all_to_all(
        sent_second.astype(jnp.bfloat16), "expert", split_axis=0, concat_axis=0, tiled=True
    ).astype(sent_second.dtype)
    flat_targets = arrived_targets.reshape(-1)
    landing = jnp.where(flat_targets >= 0, flat_targets, owned_rows)
    first_moment = (
        jnp.zeros((owned_rows, width), jnp.float32)
        .at[landing]
        .set(first_rows.reshape(-1, width), mode="drop")
    )
    second_moment = (
        jnp.zeros((owned_rows, width), jnp.float32)
        .at[landing]
        .set(second_rows.reshape(-1, width), mode="drop")
    )
    first_moment, second_moment = (
        first_moment.reshape(exp_dev, share_rows, width),
        second_moment.reshape(exp_dev, share_rows, width),
    )
    replicas = lax.axis_size("dp")
    grad_terms = grad_parts[0].reshape(exp_dev, replicas, share_rows, width)
    grad_terms = lax.all_to_all(grad_terms, "dp", split_axis=1, concat_axis=1, tiled=True)
    grad_share = jnp.sum(grad_terms.astype(jnp.float32), axis=1)
    first_new = beta_one * first_moment + (1.0 - beta_one) * grad_share
    second_new = beta_two * second_moment + (1.0 - beta_two) * grad_share * grad_share
    direction = first_new / (jnp.sqrt(second_new) + adam_eps)
    code_first, new_scale_first = quantize(first_new, block_count)
    code_second, new_scale_second = quantize(second_new, block_count)
    return (
        direction,
        jnp.stack([code_first, code_second]),
        jnp.stack([new_scale_first, new_scale_second]),
    )


def iota(shape, dim):
    return lax.broadcasted_iota(jnp.int32, shape, dim)


def dot(a, b, dims=((1,), (0,))):
    return lax.dot_general(a, b, (dims, ((), ())), preferred_element_type=f32)


def pick(rows, chosen, vector):
    return jnp.sum(jnp.where(chosen, vector, 0.0), axis=1, keepdims=True)


def resume_kernel(
    grad_ref,
    m_ref,
    v_ref,
    ms_ref,
    vs_ref,
    map_ref,
    expert_ref,
    row_ref,
    count_ref,
    offset_ref,
    dir_ref,
    codes_ref,
    scales_ref,
    flag_ref,
    old,
    moments,
    relay,
    extra,
    extra_core,
    extra_y,
    extra_z,
    part_core,
    part_y,
    send,
    recv,
    meta_send,
    meta_recv,
    grads,
    total_grad,
    place,
    late,
    wide_scales,
    load_sem,
    send_sem,
    recv_sem,
    meta_ssem,
    meta_rsem,
    grad_ssem,
    grad_rsem,
    core_sem,
    y_ssem,
    y_rsem,
    z_ssem,
    z_rsem,
):
    d = lax.axis_index("dp")
    e = lax.axis_index("expert")
    z, y, k = lax.div(e, 8), lax.rem(lax.div(e, 2), 4), lax.rem(e, 2)
    share = grads.shape[2]
    owned = 4 * share
    slots = old.shape[0]

    def peer(i):
        pz = lax.rem(z + lax.div(i, 8), 8)
        py = lax.rem(y + lax.rem(lax.div(i, 2), 4), 4)
        pk = lax.rem(k + lax.rem(i, 2), 2)
        return pz * 8 + py * 2 + pk

    def load(p, q):
        source = (m_ref, v_ref)[q // 2]
        return pltpu.make_async_copy(
            source.at[:, pl.ds((q % 2) * 1024 + p * 512, 512)],
            old.at[:, pl.ds(q * 1024 + p * 512, 512)],
            load_sem.at[p * 4 + q],
        )

    for p in range(2):
        for q in range(4):
            load(p, q).start()

    barrier = pltpu.get_barrier_semaphore()

    def greet(i, carry):
        pl.semaphore_signal(barrier, inc=1, device_id=(d, peer(i)), device_id_type=MESH)
        return carry

    for dx in range(1, 4):
        pl.semaphore_signal(
            barrier, inc=1, device_id=(lax.rem(d + dx, 4), e), device_id_type=MESH
        )
    lax.fori_loop(1, 64, greet, 0)

    count = count_ref[...].astype(f32)
    offset = offset_ref[...].astype(f32)
    unit = (iota((16, 16), 0) == iota((16, 16), 1)).astype(bf16)
    columns = (dot(ms_ref[...], unit, ((0,), (0,))), dot(vs_ref[...], unit, ((0,), (0,))))

    row, col = iota((512, 64), 0), iota((512, 64), 1)
    chosen = (row >> 3) == col
    s = (iota((512, 1), 0) & 3).astype(f32)
    source = jnp.where(s < pick(512, chosen, count), pick(512, chosen, offset) + s, -1.0)
    take = (iota((512, slots), 1).astype(f32) == source).astype(bf16)
    low = (iota((512, 256), 0) & 7) < 4

    def dequantize_half(p):
        for q in range(4):
            load(p, q).wait()
        for q in range(4):
            for b in range(4):
                block = (q % 2) * 8 + p * 4 + b
                lanes = slice(q * 1024 + p * 512 + b * 128, q * 1024 + p * 512 + (b + 1) * 128)
                moments[:, lanes] = (
                    old[:, lanes].astype(f32) * columns[q // 2][:, block : block + 1]
                ).astype(bf16)

    def pack(p):
        for c in range(2 * p, 2 * p + 2):
            quarter = [
                dot(take, moments[:, q * 1024 + c * 256 : q * 1024 + (c + 1) * 256])
                for q in range(4)
            ]
            upper = jnp.where(low, quarter[0], quarter[1]).reshape(64, 8, 256)
            lower = jnp.where(low, quarter[2], quarter[3]).reshape(64, 8, 256)
            send[p, :, :, (c % 2) * 256 : (c % 2 + 1) * 256] = jnp.concatenate(
                [upper, lower], axis=1
            ).astype(bf16)

    dequantize_half(0)
    pack(0)

    pl.semaphore_wait(barrier, 66)

    def grad_copy(dx):
        to = lax.rem(d + dx, 4)
        return pltpu.make_async_remote_copy(
            src_ref=grad_ref.at[0, :, pl.ds(pl.multiple_of(to * share, 16), share), :],
            dst_ref=grads.at[dx],
            send_sem=grad_ssem.at[dx],
            recv_sem=grad_rsem.at[dx],
            device_id=(to, e),
            device_id_type=MESH,
        )

    own_grad = pltpu.make_async_copy(
        grad_ref.at[0, :, pl.ds(pl.multiple_of(d * share, 16), share), :], grads.at[0], grad_ssem.at[0]
    )

    def meta_copy(i):
        to = peer(i)
        return pltpu.make_async_remote_copy(
            src_ref=meta_send.at[pl.ds(to, 1)],
            dst_ref=meta_recv.at[pl.ds(i, 1)],
            send_sem=meta_ssem.at[i],
            recv_sem=meta_rsem.at[i],
            device_id=(d, to),
            device_id_type=MESH,
        )

    def main_copy(p, i):
        to = peer(i)
        return pltpu.make_async_remote_copy(
            src_ref=send.at[p, to],
            dst_ref=recv.at[p, i],
            send_sem=send_sem.at[p, i],
            recv_sem=recv_sem.at[p, i],
            device_id=(d, to),
            device_id_type=MESH,
        )

    def start_meta(i, carry):
        meta_copy(i).start()
        return carry

    def wait_meta(i, carry):
        meta_copy(i).wait()
        return carry

    def start_main(p):
        def start(i, carry):
            main_copy(p, i).start()
            return carry

        return start

    def wait_main(p):
        def wait(i, carry):
            main_copy(p, i).wait()
            return carry

        return wait

    for dx in range(1, 4):
        grad_copy(dx).start()
    own_grad.start()
    lax.fori_loop(24, 64, start_main(0), 0)
    lax.fori_loop(1, 24, start_main(0), 0)
    recv[0, 0] = send[0, e]

    dequantize_half(1)
    row, col = iota((64 * EXTRA, 64), 0), iota((64 * EXTRA, 64), 1)
    u = row & 63
    owner = ((u & 7) << 3) | (((u >> 3) & 3) << 1) | (u >> 5)
    chosen = owner == col
    s = (iota((64 * EXTRA, 1), 0) >> 6).astype(f32) + float(BASE)
    source = jnp.where(
        s < pick(64 * EXTRA, chosen, count), pick(64 * EXTRA, chosen, offset) + s, -1.0
    )
    take_extra = (iota((64 * EXTRA, slots), 1).astype(f32) == source).astype(bf16)
    for c in range(8):
        rows = dot(take_extra, moments[:, c * 512 : (c + 1) * 512])
        for s_i in range(EXTRA):
            for q in range(4):
                relay[pl.ds(s_i * 32 + c * 4 + q, 64, stride=32 * EXTRA), :] = rows[
                    s_i * 64 : (s_i + 1) * 64, q * 128 : (q + 1) * 128
                ]

    def narrow(u, carry):
        extra[u] = relay[pl.ds(pl.multiple_of(u * 32 * EXTRA, 32), 32 * EXTRA), :].astype(bf16)
        return carry

    lax.fori_loop(0, 64, narrow, 0)

    core_copy = pltpu.make_async_remote_copy(
        src_ref=extra.at[pl.ds((1 - k) * 32, 32)],
        dst_ref=extra_core,
        send_sem=core_sem.at[0],
        recv_sem=core_sem.at[1],
        device_id=(d, peer(1)),
        device_id_type=MESH,
    )
    core_copy.start()
    pack(1)
    core_copy.wait()

    def add_core(g, carry):
        part_core[g] = extra[k * 32 + g] + extra_core[g]
        return carry

    lax.fori_loop(0, 32, add_core, 0)

    def y_copy(dy):
        to = lax.rem(y + dy, 4)
        return pltpu.make_async_remote_copy(
            src_ref=part_core.at[pl.ds(to * 8, 8)],
            dst_ref=extra_y.at[dy - 1],
            send_sem=y_ssem.at[dy - 1],
            recv_sem=y_rsem.at[dy - 1],
            device_id=(d, z * 8 + to * 2 + k),
            device_id_type=MESH,
        )

    def z_copy(dz):
        to = lax.rem(z + dz, 8)
        return pltpu.make_async_remote_copy(
            src_ref=part_y.at[to],
            dst_ref=extra_z.at[dz - 1],
            send_sem=z_ssem.at[dz - 1],
            recv_sem=z_rsem.at[dz - 1],
            device_id=(d, to * 8 + y * 2 + k),
            device_id_type=MESH,
        )

    for dy in range(1, 4):
        y_copy(dy).start()
    lax.fori_loop(24, 48, start_main(1), 0)

    orow, ocol = iota((64, 64), 0), iota((64, 64), 1)
    count_col = pick(64, orow == ocol, count)
    offset_col = pick(64, orow == ocol, offset)
    lane = iota((64, slots), 1).astype(f32)
    held = jnp.logical_and(lane >= offset_col, lane < offset_col + count_col)
    rank = iota((1, slots), 1).astype(f32) - jnp.sum(
        jnp.where(held, offset_col, 0.0), axis=0, keepdims=True
    )
    old_place = iota((256, slots), 0) == expert_ref[...]
    mapped = dot(
        jnp.broadcast_to(map_ref[...].astype(f32), (8, 256)).astype(bf16), old_place.astype(bf16)
    )[0:1]
    land = (mapped - 4.0 * jnp.floor(mapped * 0.25)) * float(share) + row_ref[...].astype(f32) + 1.0
    held_land = jnp.where(held, land, 0.0).astype(bf16)
    at_rank = (iota((128, slots), 0).astype(f32) == rank).astype(bf16)
    targets = dot(held_land, at_rank, ((1,), (1,)))
    shift = (iota((64, 128), 0) + 64 == iota((64, 128), 1)).astype(bf16)
    counts = dot(jnp.broadcast_to(count, (64, 64)).astype(bf16), shift)
    meta_send[...] = jnp.where(iota((64, 128), 1) < 16, targets, counts)

    for dy in range(1, 4):
        y_copy(dy).wait()

    def add_y(g, carry):
        part_y[g] = part_core[y * 8 + g] + (extra_y[0, g] + (extra_y[1, g] + extra_y[2, g]))
        return carry

    lax.fori_loop(0, 8, add_y, 0)
    for dz in range(1, 8):
        z_copy(dz).start()
    lax.fori_loop(48, 64, start_main(1), 0)
    lax.fori_loop(1, 24, start_main(1), 0)
    lax.fori_loop(1, 64, start_meta, 0)

    recv[1, 0] = send[1, e]
    meta_recv[pl.ds(0, 1), :] = meta_send[pl.ds(e, 1), :]

    own_grad.wait()
    for dx in range(1, 4):
        grad_copy(dx).wait()
    for ex in range(4):
        total_grad[ex] = (grads[0, ex].astype(f32) + grads[1, ex].astype(f32)) + (
            grads[2, ex].astype(f32) + grads[3, ex].astype(f32)
        )

    lax.fori_loop(1, 64, wait_meta, 0)
    meta = meta_recv[...]

    heavy = jnp.sum((meta > float(BASE)).astype(f32), axis=0, keepdims=True)
    heavy = jnp.where(iota((1, 128), 1) >= 64, heavy, 0.0)
    flag_ref[0] = jnp.max(heavy).astype(jnp.int32)

    spread = (iota((64, 1024), 0) == (iota((64, 1024), 1) >> 4)).astype(bf16)
    by_slot = dot(meta.astype(bf16), spread, ((0,), (0,)))[0:8]
    lane = iota((1, 1024), 1)
    goal = jnp.sum(
        jnp.where(iota((8, 1024), 0) == (lane & 3), by_slot, 0.0), axis=0, keepdims=True
    )
    hit = iota((owned, 1024), 0).astype(f32) + 1.0 == goal
    for q in range(4):
        place[q * owned : (q + 1) * owned, :] = jnp.where(
            jnp.logical_and(hit, ((lane >> 2) & 3) == q), 1.0, 0.0
        ).astype(bf16)
    late_goal = jnp.sum(meta, axis=0, keepdims=True)
    late_lane = iota((owned, 128), 1)
    late_hit = jnp.logical_and(
        iota((owned, 128), 0).astype(f32) + 1.0 == late_goal,
        jnp.logical_and(late_lane >= BASE, late_lane < BASE + EXTRA),
    )
    late_place = jnp.where(late_hit, 1.0, 0.0).astype(bf16)[:, :16]

    for dz in range(1, 8):
        z_copy(dz).wait()
    late[...] = jnp.zeros_like(late)
    total = part_y[z].astype(f32)
    for dz in range(1, 8):
        total = total + extra_z[dz - 1].astype(f32)
    late[BASE * 32 : (BASE + EXTRA) * 32, :] = total

    def unpack(p):
        for c in range(2):
            arrived = dot(
                place[...], recv[p, :, :, c * 256 : (c + 1) * 256].reshape(1024, 256)
            )
            for q in range(4):
                for b in range(2):
                    block = p * 4 + c * 2 + b
                    rest = late[pl.ds(q * 8 + block, 16, stride=32), :].astype(bf16)
                    relay[(q * 8 + block) * owned : (q * 8 + block + 1) * owned, :] = arrived[
                        q * owned : (q + 1) * owned, b * 128 : (b + 1) * 128
                    ] + dot(late_place, rest)

    def update(p):
        def one(ex, carry):
            scale_lane = iota((share, 16), 1)
            m_scales = wide_scales[0, ex]
            v_scales = wide_scales[1, ex]
            for b in [h * 8 + p * 4 + i for h in range(2) for i in range(4)]:
                at = pl.ds(pl.multiple_of(ex * share, 16) + b * owned, share)
                at_v = pl.ds(pl.multiple_of(ex * share, 16) + (16 + b) * owned, share)
                out = slice(b * 128, (b + 1) * 128)
                g = total_grad[ex, :, out]
                m = beta_one * relay[at, :] + (1.0 - beta_one) * g
                v = beta_two * relay[at_v, :] + (1.0 - beta_two) * g * g
                dir_ref[ex, :, out] = m / (jnp.sqrt(v) + adam_eps)
                m_scale = (jnp.max(jnp.abs(m), axis=1, keepdims=True) + scale_eps).astype(bf16)
                v_scale = (jnp.max(jnp.abs(v), axis=1, keepdims=True) + scale_eps).astype(bf16)
                m_wide, v_wide = m_scale.astype(f32), v_scale.astype(f32)
                codes_ref[0, ex, :, out] = (m * (1.0 / m_wide)).astype(bf16)
                codes_ref[1, ex, :, out] = (v * (1.0 / v_wide)).astype(bf16)
                m_scales = jnp.where(scale_lane == b, m_wide, m_scales)
                v_scales = jnp.where(scale_lane == b, v_wide, v_scales)
            wide_scales[0, ex] = m_scales
            wide_scales[1, ex] = v_scales
            return carry

        lax.fori_loop(0, 4, one, 0)

    wide_scales[...] = jnp.zeros_like(wide_scales)
    lax.fori_loop(1, 64, wait_main(0), 0)
    unpack(0)
    update(0)
    lax.fori_loop(1, 64, wait_main(1), 0)
    unpack(1)
    update(1)
    turn = (iota((share, share), 0) == iota((share, share), 1)).astype(bf16)
    for part in range(2):
        for ex in range(4):
            scales_ref[part, ex] = dot(
                wide_scales[part, ex].astype(bf16), turn, ((0,), (0,))
            ).astype(bf16)


def exchange(grad_parts, m_codes, v_codes, m_scale, v_scale, expert_map, slot_expert, slot_row, count, offset):
    slots, width, blocks = m_codes.shape[2], m_codes.shape[3], m_scale.shape[3]
    share = grad_parts.shape[2] // 4
    owned = 4 * share
    vmem = pl.BlockSpec(memory_space=pltpu.VMEM)
    hbm = pl.BlockSpec(memory_space=pl.ANY)
    chunk = 32 * EXTRA
    direction, codes, scales, heavy = pl.pallas_call(
        resume_kernel,
        out_shape=(
            jax.ShapeDtypeStruct((4, share, width), f32),
            jax.ShapeDtypeStruct((2, 4, share, width), bf16),
            jax.ShapeDtypeStruct((2, 4, blocks, share), bf16),
            jax.ShapeDtypeStruct((1,), jnp.int32),
        ),
        in_specs=[hbm] * 3 + [vmem] * 7,
        out_specs=(vmem,) * 3 + (pl.BlockSpec(memory_space=pltpu.SMEM),),
        scratch_shapes=[
            pltpu.VMEM((slots, 2 * width), bf16),
            pltpu.VMEM((slots, 2 * width), bf16),
            pltpu.VMEM((64 * chunk, 128), f32),
            pltpu.VMEM((64, chunk, 128), bf16),
            pltpu.VMEM((32, chunk, 128), bf16),
            pltpu.VMEM((3, 8, chunk, 128), bf16),
            pltpu.VMEM((7, chunk, 128), bf16),
            pltpu.VMEM((32, chunk, 128), bf16),
            pltpu.VMEM((8, chunk, 128), bf16),
            pltpu.VMEM((2, 64, 16, 512), bf16),
            pltpu.VMEM((2, 64, 16, 512), bf16),
            pltpu.VMEM((64, 128), f32),
            pltpu.VMEM((64, 128), f32),
            pltpu.VMEM((4, 4, share, width), bf16),
            pltpu.VMEM((4, share, width), f32),
            pltpu.VMEM((4 * owned, 1024), bf16),
            pltpu.VMEM((16 * 32, 128), f32),
            pltpu.VMEM((2, 4, share, 16), f32),
            pltpu.SemaphoreType.DMA((8,)),
            pltpu.SemaphoreType.DMA((2, 64)),
            pltpu.SemaphoreType.DMA((2, 64)),
            pltpu.SemaphoreType.DMA((64,)),
            pltpu.SemaphoreType.DMA((64,)),
            pltpu.SemaphoreType.DMA((4,)),
            pltpu.SemaphoreType.DMA((4,)),
            pltpu.SemaphoreType.DMA((2,)),
            pltpu.SemaphoreType.DMA((3,)),
            pltpu.SemaphoreType.DMA((3,)),
            pltpu.SemaphoreType.DMA((7,)),
            pltpu.SemaphoreType.DMA((7,)),
        ],
        compiler_params=pltpu.CompilerParams(
            collective_id=0, has_side_effects=True, vmem_limit_bytes=VMEM_MIB * 2**20
        ),
        name="resume",
    )(
        grad_parts,
        m_codes[0, 0],
        v_codes[0, 0],
        m_scale[0, 0].T,
        v_scale[0, 0].T,
        expert_map.reshape(1, -1),
        slot_expert,
        slot_row,
        count,
        offset,
    )
    return direction, codes, jnp.swapaxes(scales, 2, 3), heavy


def per_device(*args):
    direction, codes, scales, heavy = exchange(*args)
    return lax.cond(
        heavy[0] < 2,
        lambda: (direction, codes, scales),
        lambda: padded_exchange(*args),
    )


def solution(mesh):
    in_specs = (
        P("dp", "expert", None, None),
        P("dp", "expert", None, None),
        P("dp", "expert", None, None),
        P("dp", "expert", None, None),
        P("dp", "expert", None, None),
        P(),
        P("expert", None),
        P("expert", None),
        P("expert", None),
        P("expert", None),
    )
    out_specs = (
        P("expert", "dp", None),
        P(None, "expert", "dp", None),
        P(None, "expert", "dp", None),
    )
    return jax.shard_map(
        per_device, mesh=mesh, in_specs=in_specs, out_specs=out_specs, check_vma=False
    )
```

```python
import functools

import jax
import jax.numpy as jnp
from jax import lax
from jax.experimental import pallas as pl
from jax.experimental.pallas import tpu as pltpu
from jax.sharding import PartitionSpec as P

beta_one = 0.9
beta_two = 0.95
adam_eps = 1e-08
scale_eps = 1e-06

MESH = pl.DeviceIdType.MESH
f32 = jnp.float32
bf16 = jnp.bfloat16
BASE = 4
EXTRA = 5
VMEM_MIB = 44


def dequantize(code_array, block_scale):
    full_shape = code_array.shape
    blocks = code_array.astype(jnp.float32).reshape(
        full_shape[:-1] + (block_scale.shape[-1], full_shape[-1] // block_scale.shape[-1])
    )
    return (blocks * block_scale.astype(jnp.float32)[..., None]).reshape(full_shape)


def quantize(values, block_count):
    full_shape = values.shape
    blocks = values.reshape(full_shape[:-1] + (block_count, full_shape[-1] // block_count))
    block_scale = (jnp.max(jnp.abs(blocks), axis=-1) + scale_eps).astype(jnp.bfloat16)
    code_array = (blocks / block_scale.astype(jnp.float32)[..., None]).astype(jnp.bfloat16)
    return (code_array.reshape(full_shape), block_scale)


def padded_exchange(
    grad_parts,
    old_m_codes,
    old_v_codes,
    old_m_scale,
    old_v_scale,
    expert_map,
    slot_expert,
    slot_row,
    peer_count,
    peer_offset,
):
    owners = lax.axis_size("expert")
    codes_first = old_m_codes[0, 0]
    codes_second = old_v_codes[0, 0]
    scale_first = old_m_scale[0, 0]
    scale_second = old_v_scale[0, 0]
    slot_total = codes_first.shape[0]
    width = codes_first.shape[1]
    block_count = scale_first.shape[1]
    per_peer = slot_total // owners
    exp_dev = grad_parts.shape[1]
    share_rows = grad_parts.shape[2] // lax.axis_size("dp")
    owned_rows = exp_dev * share_rows
    send_counts = peer_count[0]
    offsets = peer_offset[0]
    slot_place = jnp.arange(per_peer, dtype=jnp.int32)[None, :]
    picked = (offsets[:, None] + slot_place).reshape(-1)
    new_expert = expert_map[slot_expert[0]]
    local_all = new_expert % exp_dev * share_rows + slot_row[0]
    usable = slot_place < send_counts[:, None]
    targets = jnp.where(usable, local_all[picked].reshape(owners, per_peer), -1)
    arrived_targets = lax.all_to_all(targets, "expert", split_axis=0, concat_axis=0, tiled=True)
    sent_first = dequantize(codes_first[picked], scale_first[picked]).reshape(
        owners, per_peer, width
    )
    sent_second = dequantize(codes_second[picked], scale_second[picked]).reshape(
        owners, per_peer, width
    )
    first_rows = lax.all_to_all(
        sent_first.astype(jnp.bfloat16), "expert", split_axis=0, concat_axis=0, tiled=True
    ).astype(sent_first.dtype)
    second_rows = lax.all_to_all(
        sent_second.astype(jnp.bfloat16), "expert", split_axis=0, concat_axis=0, tiled=True
    ).astype(sent_second.dtype)
    flat_targets = arrived_targets.reshape(-1)
    landing = jnp.where(flat_targets >= 0, flat_targets, owned_rows)
    first_moment = (
        jnp.zeros((owned_rows, width), jnp.float32)
        .at[landing]
        .set(first_rows.reshape(-1, width), mode="drop")
    )
    second_moment = (
        jnp.zeros((owned_rows, width), jnp.float32)
        .at[landing]
        .set(second_rows.reshape(-1, width), mode="drop")
    )
    first_moment, second_moment = (
        first_moment.reshape(exp_dev, share_rows, width),
        second_moment.reshape(exp_dev, share_rows, width),
    )
    replicas = lax.axis_size("dp")
    grad_terms = grad_parts[0].reshape(exp_dev, replicas, share_rows, width)
    grad_terms = lax.all_to_all(grad_terms, "dp", split_axis=1, concat_axis=1, tiled=True)
    grad_share = jnp.sum(grad_terms.astype(jnp.float32), axis=1)
    first_new = beta_one * first_moment + (1.0 - beta_one) * grad_share
    second_new = beta_two * second_moment + (1.0 - beta_two) * grad_share * grad_share
    direction = first_new / (jnp.sqrt(second_new) + adam_eps)
    code_first, new_scale_first = quantize(first_new, block_count)
    code_second, new_scale_second = quantize(second_new, block_count)
    return (
        direction,
        jnp.stack([code_first, code_second]),
        jnp.stack([new_scale_first, new_scale_second]),
    )


def iota(shape, dim):
    return lax.broadcasted_iota(jnp.int32, shape, dim)


def dot(a, b, dims=((1,), (0,))):
    return lax.dot_general(a, b, (dims, ((), ())), preferred_element_type=f32)


def pick(rows, chosen, vector):
    return jnp.sum(jnp.where(chosen, vector, 0.0), axis=1, keepdims=True)


def resume_kernel(
    grad_ref,
    m_ref,
    v_ref,
    ms_ref,
    vs_ref,
    map_ref,
    expert_ref,
    row_ref,
    count_ref,
    offset_ref,
    dir_ref,
    codes_ref,
    scales_ref,
    flag_ref,
    old,
    moments,
    relay,
    extra,
    extra_core,
    extra_y,
    extra_z,
    part_core,
    part_y,
    send,
    recv,
    land_own,
    land_plane,
    land_part,
    land_z,
    grads,
    total_grad,
    place,
    late,
    wide_scales,
    dir_out,
    codes_out,
    load_sem,
    store_sem,
    send_sem,
    recv_sem,
    land_ssem,
    land_rsem,
    grad_ssem,
    grad_rsem,
    core_sem,
    y_ssem,
    y_rsem,
    z_ssem,
    z_rsem,
    ready,
):
    d = lax.axis_index("dp")
    e = lax.axis_index("expert")
    z, y, k = lax.div(e, 8), lax.rem(lax.div(e, 2), 4), lax.rem(e, 2)
    share = grads.shape[2]
    owned = 4 * share
    slots = old.shape[0]

    def peer(i):
        pz = lax.rem(z + lax.div(i, 8), 8)
        py = lax.rem(y + lax.rem(lax.div(i, 2), 4), 4)
        pk = lax.rem(k + lax.rem(i, 2), 2)
        return pz * 8 + py * 2 + pk

    def load(p, q):
        source = (m_ref, v_ref)[q // 2]
        return pltpu.make_async_copy(
            source.at[:, pl.ds((q % 2) * 1024 + p * 512, 512)],
            old.at[:, pl.ds(q * 1024 + p * 512, 512)],
            load_sem.at[p * 4 + q],
        )

    for p in range(2):
        for q in range(4):
            load(p, q).start()

    barrier = pltpu.get_barrier_semaphore()

    for i in list(range(1, 8)) + list(range(8, 64, 8)):
        pl.semaphore_signal(barrier, inc=1, device_id=(d, peer(i)), device_id_type=MESH)
    for dx in range(1, 4):
        pl.semaphore_signal(
            barrier, inc=1, device_id=(lax.rem(d + dx, 4), e), device_id_type=MESH
        )

    count = count_ref[...].astype(f32)
    offset = offset_ref[...].astype(f32)
    unit = (iota((16, 16), 0) == iota((16, 16), 1)).astype(bf16)
    columns = (dot(ms_ref[...], unit, ((0,), (0,))), dot(vs_ref[...], unit, ((0,), (0,))))

    row, col = iota((512, 64), 0), iota((512, 64), 1)
    chosen = (row >> 3) == col
    s = (iota((512, 1), 0) & 3).astype(f32)
    source = jnp.where(s < pick(512, chosen, count), pick(512, chosen, offset) + s, -1.0)
    take = (iota((512, slots), 1).astype(f32) == source).astype(bf16)
    low = (iota((512, 256), 0) & 7) < 4

    def dequantize_half(p):
        for q in range(4):
            load(p, q).wait()
        for q in range(4):
            for b in range(4):
                block = (q % 2) * 8 + p * 4 + b
                lanes = slice(q * 1024 + p * 512 + b * 128, q * 1024 + p * 512 + (b + 1) * 128)
                moments[:, lanes] = (
                    old[:, lanes].astype(f32) * columns[q // 2][:, block : block + 1]
                ).astype(bf16)

    def pack(p):
        for c in range(2 * p, 2 * p + 2):
            quarter = [
                dot(take, moments[:, q * 1024 + c * 256 : q * 1024 + (c + 1) * 256])
                for q in range(4)
            ]
            upper = jnp.where(low, quarter[0], quarter[1]).reshape(64, 8, 256)
            lower = jnp.where(low, quarter[2], quarter[3]).reshape(64, 8, 256)
            send[p, :, :, (c % 2) * 256 : (c % 2 + 1) * 256] = jnp.concatenate(
                [upper, lower], axis=1
            ).astype(bf16)

    def remote(source, target, send_s, recv_s, to):
        return pltpu.make_async_remote_copy(
            src_ref=source,
            dst_ref=target,
            send_sem=send_s,
            recv_sem=recv_s,
            device_id=(d, to),
            device_id_type=MESH,
        )

    def land_plane_copy(i):
        to = peer(i)
        return remote(
            land_own.at[pl.ds(pl.multiple_of(lax.rem(to, 8) * 8, 8), 8)],
            land_plane.at[i],
            land_ssem.at[i],
            land_rsem.at[i],
            to,
        )

    def land_z_copy(dz):
        to = lax.rem(z + dz, 8)
        return remote(
            land_part.at[pl.ds(to, 1)],
            land_z.at[pl.ds(dz, 1)],
            land_ssem.at[8 + dz],
            land_rsem.at[8 + dz],
            to * 8 + y * 2 + k,
        )

    urow, ocol = iota((64, 64), 0), iota((64, 64), 1)
    mine = (((urow & 7) << 3) | (urow >> 3)) == ocol
    count_col = pick(64, mine, count)
    offset_col = pick(64, mine, offset)
    lane = iota((64, slots), 1).astype(f32)
    held = jnp.logical_and(lane >= offset_col, lane < offset_col + count_col)
    rank = iota((1, slots), 1).astype(f32) - jnp.sum(
        jnp.where(held, offset_col, 0.0), axis=0, keepdims=True
    )
    old_place = iota((256, slots), 0) == expert_ref[...]
    mapped = dot(
        jnp.broadcast_to(map_ref[...].astype(f32), (8, 256)).astype(bf16), old_place.astype(bf16)
    )[0:1]
    land = (mapped - 4.0 * jnp.floor(mapped * 0.25)) * float(share) + row_ref[...].astype(f32) + 1.0
    held_land = jnp.where(held, land, 0.0).astype(bf16)
    at_rank = (iota((128, slots), 0).astype(f32) == rank).astype(bf16)
    targets = dot(held_land, at_rank, ((1,), (1,)))
    slot, lane = iota((128, 384), 0), iota((128, 384), 1)
    first = jnp.logical_and(slot < BASE, lane == e * BASE + slot)
    later = jnp.logical_and(slot >= BASE, lane == 256 + slot - BASE)
    keep = jnp.where(jnp.logical_or(first, later), 1.0, 0.0).astype(bf16)
    tell = (iota((64, 384), 0) + 320 == iota((64, 384), 1)).astype(bf16)
    heavy = jnp.broadcast_to((count > float(BASE)).astype(f32), (64, 64)).astype(bf16)
    land_own[...] = dot(targets.astype(bf16), keep) + dot(heavy, tell)

    dequantize_half(0)
    pl.semaphore_wait(barrier, 17)
    for i in range(1, 8):
        pl.semaphore_signal(ready, inc=1, device_id=(d, peer(i)), device_id_type=MESH)
    for i in range(1, 8):
        land_plane_copy(i).start()
    pack(0)
    for i in range(1, 8):
        land_plane_copy(i).wait()
    land_plane[0] = land_own[pl.ds(pl.multiple_of(lax.rem(e, 8) * 8, 8), 8), :]
    land_part[...] = jnp.sum(land_plane[...], axis=0)
    for dz in range(1, 8):
        land_z_copy(dz).start()
    land_z[pl.ds(0, 1), :] = land_part[pl.ds(z, 1), :]
    pl.semaphore_wait(ready, 7)

    def grad_copy(dx):
        to = lax.rem(d + dx, 4)
        return pltpu.make_async_remote_copy(
            src_ref=grad_ref.at[0, :, pl.ds(pl.multiple_of(to * share, 16), share), :],
            dst_ref=grads.at[dx],
            send_sem=grad_ssem.at[dx],
            recv_sem=grad_rsem.at[dx],
            device_id=(to, e),
            device_id_type=MESH,
        )

    own_grad = pltpu.make_async_copy(
        grad_ref.at[0, :, pl.ds(pl.multiple_of(d * share, 16), share), :], grads.at[0], grad_ssem.at[0]
    )

    def main_copy(p, i):
        to = peer(i)
        return remote(send.at[p, to], recv.at[p, e], send_sem.at[p, to], recv_sem.at[p, e], to)

    def main_arrival(p, i):
        to = peer(i)
        return remote(send.at[p, to], recv.at[p, to], send_sem.at[p, to], recv_sem.at[p, to], to)

    def start_main(p):
        def start(i, carry):
            main_copy(p, i).start()
            return carry

        return start

    def wait_main(p):
        def wait(i, carry):
            main_arrival(p, i).wait()
            return carry

        return wait

    for dx in range(1, 4):
        grad_copy(dx).start()
    own_grad.start()
    lax.fori_loop(24, 64, start_main(0), 0)
    lax.fori_loop(1, 24, start_main(0), 0)
    recv[0, e] = send[0, e]

    dequantize_half(1)
    row, col = iota((64 * EXTRA, 64), 0), iota((64 * EXTRA, 64), 1)
    u = row & 63
    owner = ((u & 7) << 3) | (((u >> 3) & 3) << 1) | (u >> 5)
    chosen = owner == col
    s = (iota((64 * EXTRA, 1), 0) >> 6).astype(f32) + float(BASE)
    source = jnp.where(
        s < pick(64 * EXTRA, chosen, count), pick(64 * EXTRA, chosen, offset) + s, -1.0
    )
    take_extra = (iota((64 * EXTRA, slots), 1).astype(f32) == source).astype(bf16)
    for c in range(8):
        rows = dot(take_extra, moments[:, c * 512 : (c + 1) * 512])
        for s_i in range(EXTRA):
            for q in range(4):
                relay[pl.ds(s_i * 32 + c * 4 + q, 64, stride=32 * EXTRA), :] = rows[
                    s_i * 64 : (s_i + 1) * 64, q * 128 : (q + 1) * 128
                ]

    def narrow(u, carry):
        extra[u] = relay[pl.ds(pl.multiple_of(u * 32 * EXTRA, 32), 32 * EXTRA), :].astype(bf16)
        return carry

    lax.fori_loop(0, 64, narrow, 0)

    core_copy = pltpu.make_async_remote_copy(
        src_ref=extra.at[pl.ds((1 - k) * 32, 32)],
        dst_ref=extra_core,
        send_sem=core_sem.at[0],
        recv_sem=core_sem.at[1],
        device_id=(d, peer(1)),
        device_id_type=MESH,
    )
    core_copy.start()
    pack(1)
    core_copy.wait()

    def add_core(g, carry):
        part_core[g] = extra[k * 32 + g] + extra_core[g]
        return carry

    lax.fori_loop(0, 32, add_core, 0)

    def y_copy(dy):
        to = lax.rem(y + dy, 4)
        return pltpu.make_async_remote_copy(
            src_ref=part_core.at[pl.ds(to * 8, 8)],
            dst_ref=extra_y.at[dy - 1],
            send_sem=y_ssem.at[dy - 1],
            recv_sem=y_rsem.at[dy - 1],
            device_id=(d, z * 8 + to * 2 + k),
            device_id_type=MESH,
        )

    def z_copy(dz):
        to = lax.rem(z + dz, 8)
        return pltpu.make_async_remote_copy(
            src_ref=part_y.at[to],
            dst_ref=extra_z.at[dz - 1],
            send_sem=z_ssem.at[dz - 1],
            recv_sem=z_rsem.at[dz - 1],
            device_id=(d, to * 8 + y * 2 + k),
            device_id_type=MESH,
        )

    for dy in range(1, 4):
        y_copy(dy).start()
    lax.fori_loop(24, 48, start_main(1), 0)

    for dy in range(1, 4):
        y_copy(dy).wait()

    def add_y(g, carry):
        part_y[g] = part_core[y * 8 + g] + (extra_y[0, g] + (extra_y[1, g] + extra_y[2, g]))
        return carry

    lax.fori_loop(0, 8, add_y, 0)
    for dz in range(1, 8):
        z_copy(dz).start()
    lax.fori_loop(48, 64, start_main(1), 0)
    lax.fori_loop(1, 24, start_main(1), 0)

    recv[1, e] = send[1, e]

    own_grad.wait()
    for dx in range(1, 4):
        grad_copy(dx).wait()
    for ex in range(4):
        total_grad[ex] = (grads[0, ex].astype(f32) + grads[1, ex].astype(f32)) + (
            grads[2, ex].astype(f32) + grads[3, ex].astype(f32)
        )

    for dz in range(1, 8):
        land_z_copy(dz).wait()
    landing = jnp.sum(land_z[...], axis=0, keepdims=True)
    flag_ref[0] = jnp.max(landing[:, 256:] * (iota((1, 128), 1) >= 64).astype(f32)).astype(jnp.int32)
    near, lane = iota((256, 1024), 0), iota((256, 1024), 1)
    spread = jnp.logical_and((near >> 2) == (lane >> 4), (near & 3) == (lane & 3))
    goal = dot(
        jnp.broadcast_to(landing[:, :256], (8, 256)).astype(bf16),
        jnp.where(spread, 1.0, 0.0).astype(bf16),
    )[0:1]
    lane = iota((1, 1024), 1)
    hit = iota((owned, 1024), 0).astype(f32) + 1.0 == goal
    for q in range(4):
        place[q * owned : (q + 1) * owned, :] = jnp.where(
            jnp.logical_and(hit, ((lane >> 2) & 3) == q), 1.0, 0.0
        ).astype(bf16)
    late_hit = jnp.logical_and(
        iota((owned, 128), 0).astype(f32) + 1.0 == landing[:, 256:], iota((owned, 128), 1) < EXTRA
    )
    late_place = jnp.where(late_hit, 1.0, 0.0).astype(bf16)[:, :16]

    for dz in range(1, 8):
        z_copy(dz).wait()
    late[...] = jnp.zeros_like(late)
    total = part_y[z].astype(f32)
    for dz in range(1, 8):
        total = total + extra_z[dz - 1].astype(f32)
    late[: EXTRA * 32, :] = total

    def unpack(p):
        for c in range(2):
            arrived = dot(
                place[...], recv[p, :, :, c * 256 : (c + 1) * 256].reshape(1024, 256)
            )
            for q in range(4):
                for b in range(2):
                    block = p * 4 + c * 2 + b
                    rest = late[pl.ds(q * 8 + block, 16, stride=32), :].astype(bf16)
                    relay[(q * 8 + block) * owned : (q * 8 + block + 1) * owned, :] = arrived[
                        q * owned : (q + 1) * owned, b * 128 : (b + 1) * 128
                    ] + dot(late_place, rest)

    def update(p):
        def one(ex, carry):
            scale_lane = iota((share, 16), 1)
            m_scales = wide_scales[0, ex]
            v_scales = wide_scales[1, ex]
            for b in [h * 8 + p * 4 + i for h in range(2) for i in range(4)]:
                at = pl.ds(pl.multiple_of(ex * share, 16) + b * owned, share)
                at_v = pl.ds(pl.multiple_of(ex * share, 16) + (16 + b) * owned, share)
                out = slice(b * 128, (b + 1) * 128)
                g = total_grad[ex, :, out]
                m = beta_one * relay[at, :] + (1.0 - beta_one) * g
                v = beta_two * relay[at_v, :] + (1.0 - beta_two) * g * g
                dir_out[ex, :, out] = m / (jnp.sqrt(v) + adam_eps)
                m_scale = (jnp.max(jnp.abs(m), axis=1, keepdims=True) + scale_eps).astype(bf16)
                v_scale = (jnp.max(jnp.abs(v), axis=1, keepdims=True) + scale_eps).astype(bf16)
                m_wide, v_wide = m_scale.astype(f32), v_scale.astype(f32)
                codes_out[0, ex, :, out] = (m * (1.0 / m_wide)).astype(bf16)
                codes_out[1, ex, :, out] = (v * (1.0 / v_wide)).astype(bf16)
                m_scales = jnp.where(scale_lane == b, m_wide, m_scales)
                v_scales = jnp.where(scale_lane == b, v_wide, v_scales)
            wide_scales[0, ex] = m_scales
            wide_scales[1, ex] = v_scales
            return carry

        lax.fori_loop(0, 4, one, 0)

    def stores(p):
        copies = []
        for h in range(2):
            lanes = pl.ds(h * 1024 + p * 512, 512)
            n = (p * 2 + h) * 2
            copies.append(
                pltpu.make_async_copy(
                    dir_out.at[:, :, lanes], dir_ref.at[:, :, lanes], store_sem.at[n]
                )
            )
            copies.append(
                pltpu.make_async_copy(
                    codes_out.at[:, :, :, lanes], codes_ref.at[:, :, :, lanes], store_sem.at[n + 1]
                )
            )
        return copies

    wide_scales[...] = jnp.zeros_like(wide_scales)
    for p in range(2):
        lax.fori_loop(1, 64, wait_main(p), 0)
        unpack(p)
        update(p)
        for copy in stores(p):
            copy.start()
    turn = (iota((share, share), 0) == iota((share, share), 1)).astype(bf16)
    for part in range(2):
        for ex in range(4):
            scales_ref[part, ex] = dot(
                wide_scales[part, ex].astype(bf16), turn, ((0,), (0,))
            ).astype(bf16)
    for p in range(2):
        for copy in stores(p):
            copy.wait()


def hand_on_kernel(dir_ref, codes_ref, scales_ref, dir_to, codes_to, scales_to, dirs, codes, scales, sem):
    pieces = [(scales_ref, scales, scales_to)]
    for ex in range(4):
        pieces.append((dir_ref.at[ex], dirs.at[ex], dir_to.at[ex]))
        for part in range(2):
            pieces.append((codes_ref.at[part, ex], codes.at[part, ex], codes_to.at[part, ex]))
    loads = [
        pltpu.make_async_copy(source, held, sem.at[0, n]) for n, (source, held, _) in enumerate(pieces)
    ]
    stores = [
        pltpu.make_async_copy(held, target, sem.at[1, n]) for n, (_, held, target) in enumerate(pieces)
    ]
    for copy in loads:
        copy.start()
    for first, second in zip(loads, stores):
        first.wait()
        second.start()
    for copy in stores:
        copy.wait()


def hand_on(*results):
    return tuple(
        pl.pallas_call(
            hand_on_kernel,
            out_shape=tuple(jax.ShapeDtypeStruct(r.shape, r.dtype) for r in results),
            in_specs=[pl.BlockSpec(memory_space=pl.ANY)] * 3,
            out_specs=(pl.BlockSpec(memory_space=pl.ANY),) * 3,
            scratch_shapes=[pltpu.VMEM(r.shape, r.dtype) for r in results]
            + [pltpu.SemaphoreType.DMA((2, 13))],
            name="hand_on",
        )(*results)
    )


def exchange(grad_parts, m_codes, v_codes, m_scale, v_scale, expert_map, slot_expert, slot_row, count, offset):
    slots, width, blocks = m_codes.shape[2], m_codes.shape[3], m_scale.shape[3]
    share = grad_parts.shape[2] // 4
    owned = 4 * share
    vmem = pl.BlockSpec(memory_space=pltpu.VMEM)
    hbm = pl.BlockSpec(memory_space=pl.ANY)
    chunk = 32 * EXTRA
    direction, codes, scales, heavy = pl.pallas_call(
        resume_kernel,
        out_shape=(
            jax.ShapeDtypeStruct((4, share, width), f32),
            jax.ShapeDtypeStruct((2, 4, share, width), bf16),
            jax.ShapeDtypeStruct((2, 4, blocks, share), bf16),
            jax.ShapeDtypeStruct((1,), jnp.int32),
        ),
        in_specs=[hbm] * 3 + [vmem] * 7,
        out_specs=(hbm, hbm, vmem, pl.BlockSpec(memory_space=pltpu.SMEM)),
        scratch_shapes=[
            pltpu.VMEM((slots, 2 * width), bf16),
            pltpu.VMEM((slots, 2 * width), bf16),
            pltpu.VMEM((64 * chunk, 128), f32),
            pltpu.VMEM((64, chunk, 128), bf16),
            pltpu.VMEM((32, chunk, 128), bf16),
            pltpu.VMEM((3, 8, chunk, 128), bf16),
            pltpu.VMEM((7, chunk, 128), bf16),
            pltpu.VMEM((32, chunk, 128), bf16),
            pltpu.VMEM((8, chunk, 128), bf16),
            pltpu.VMEM((2, 64, 16, 512), bf16),
            pltpu.VMEM((2, 64, 16, 512), bf16),
            pltpu.VMEM((64, 384), f32),
            pltpu.VMEM((8, 8, 384), f32),
            pltpu.VMEM((8, 384), f32),
            pltpu.VMEM((8, 384), f32),
            pltpu.VMEM((4, 4, share, width), bf16),
            pltpu.VMEM((4, share, width), f32),
            pltpu.VMEM((4 * owned, 1024), bf16),
            pltpu.VMEM((16 * 32, 128), f32),
            pltpu.VMEM((2, 4, share, 16), f32),
            pltpu.VMEM((4, share, width), f32),
            pltpu.VMEM((2, 4, share, width), bf16),
            pltpu.SemaphoreType.DMA((8,)),
            pltpu.SemaphoreType.DMA((8,)),
            pltpu.SemaphoreType.DMA((2, 64)),
            pltpu.SemaphoreType.DMA((2, 64)),
            pltpu.SemaphoreType.DMA((16,)),
            pltpu.SemaphoreType.DMA((16,)),
            pltpu.SemaphoreType.DMA((4,)),
            pltpu.SemaphoreType.DMA((4,)),
            pltpu.SemaphoreType.DMA((2,)),
            pltpu.SemaphoreType.DMA((3,)),
            pltpu.SemaphoreType.DMA((3,)),
            pltpu.SemaphoreType.DMA((7,)),
            pltpu.SemaphoreType.DMA((7,)),
            pltpu.SemaphoreType.REGULAR,
        ],
        compiler_params=pltpu.CompilerParams(
            collective_id=0, has_side_effects=True, vmem_limit_bytes=VMEM_MIB * 2**20
        ),
        name="resume",
    )(
        grad_parts,
        m_codes[0, 0],
        v_codes[0, 0],
        m_scale[0, 0].T,
        v_scale[0, 0].T,
        expert_map.reshape(1, -1),
        slot_expert,
        slot_row,
        count,
        offset,
    )
    return direction, codes, scales, heavy


def per_device(*args):
    direction, codes, scales, heavy = exchange(*args)

    def padded():
        direction, codes, scales = padded_exchange(*args)
        return direction, codes, jnp.swapaxes(scales, 2, 3)

    direction, codes, scales = lax.cond(
        heavy[0] < 2, lambda: hand_on(direction, codes, scales), padded
    )
    return direction, codes, jnp.swapaxes(scales, 2, 3)


def solution(mesh):
    in_specs = (
        P("dp", "expert", None, None),
        P("dp", "expert", None, None),
        P("dp", "expert", None, None),
        P("dp", "expert", None, None),
        P("dp", "expert", None, None),
        P(),
        P("expert", None),
        P("expert", None),
        P("expert", None),
        P("expert", None),
    )
    out_specs = (
        P("expert", "dp", None),
        P(None, "expert", "dp", None),
        P(None, "expert", "dp", None),
    )
    return jax.shard_map(
        per_device, mesh=mesh, in_specs=in_specs, out_specs=out_specs, check_vma=False
    )
```

```python
import functools

import jax
import jax.numpy as jnp
from jax import lax
from jax.experimental import pallas as pl
from jax.experimental.pallas import tpu as pltpu
from jax.sharding import PartitionSpec as P

beta_one = 0.9
beta_two = 0.95
adam_eps = 1e-08
scale_eps = 1e-06

MESH = pl.DeviceIdType.MESH
f32 = jnp.float32
bf16 = jnp.bfloat16
BASE = 4
EXTRA = 5
VMEM_MIB = 44


def dequantize(code_array, block_scale):
    full_shape = code_array.shape
    blocks = code_array.astype(jnp.float32).reshape(
        full_shape[:-1] + (block_scale.shape[-1], full_shape[-1] // block_scale.shape[-1])
    )
    return (blocks * block_scale.astype(jnp.float32)[..., None]).reshape(full_shape)


def quantize(values, block_count):
    full_shape = values.shape
    blocks = values.reshape(full_shape[:-1] + (block_count, full_shape[-1] // block_count))
    block_scale = (jnp.max(jnp.abs(blocks), axis=-1) + scale_eps).astype(jnp.bfloat16)
    code_array = (blocks / block_scale.astype(jnp.float32)[..., None]).astype(jnp.bfloat16)
    return (code_array.reshape(full_shape), block_scale)


def padded_exchange(
    grad_parts,
    old_m_codes,
    old_v_codes,
    old_m_scale,
    old_v_scale,
    expert_map,
    slot_expert,
    slot_row,
    peer_count,
    peer_offset,
):
    owners = lax.axis_size("expert")
    codes_first = old_m_codes[0, 0]
    codes_second = old_v_codes[0, 0]
    scale_first = old_m_scale[0, 0]
    scale_second = old_v_scale[0, 0]
    slot_total = codes_first.shape[0]
    width = codes_first.shape[1]
    block_count = scale_first.shape[1]
    per_peer = slot_total // owners
    exp_dev = grad_parts.shape[1]
    share_rows = grad_parts.shape[2] // lax.axis_size("dp")
    owned_rows = exp_dev * share_rows
    send_counts = peer_count[0]
    offsets = peer_offset[0]
    slot_place = jnp.arange(per_peer, dtype=jnp.int32)[None, :]
    picked = (offsets[:, None] + slot_place).reshape(-1)
    new_expert = expert_map[slot_expert[0]]
    local_all = new_expert % exp_dev * share_rows + slot_row[0]
    usable = slot_place < send_counts[:, None]
    targets = jnp.where(usable, local_all[picked].reshape(owners, per_peer), -1)
    arrived_targets = lax.all_to_all(targets, "expert", split_axis=0, concat_axis=0, tiled=True)
    sent_first = dequantize(codes_first[picked], scale_first[picked]).reshape(
        owners, per_peer, width
    )
    sent_second = dequantize(codes_second[picked], scale_second[picked]).reshape(
        owners, per_peer, width
    )
    first_rows = lax.all_to_all(
        sent_first.astype(jnp.bfloat16), "expert", split_axis=0, concat_axis=0, tiled=True
    ).astype(sent_first.dtype)
    second_rows = lax.all_to_all(
        sent_second.astype(jnp.bfloat16), "expert", split_axis=0, concat_axis=0, tiled=True
    ).astype(sent_second.dtype)
    flat_targets = arrived_targets.reshape(-1)
    landing = jnp.where(flat_targets >= 0, flat_targets, owned_rows)
    first_moment = (
        jnp.zeros((owned_rows, width), jnp.float32)
        .at[landing]
        .set(first_rows.reshape(-1, width), mode="drop")
    )
    second_moment = (
        jnp.zeros((owned_rows, width), jnp.float32)
        .at[landing]
        .set(second_rows.reshape(-1, width), mode="drop")
    )
    first_moment, second_moment = (
        first_moment.reshape(exp_dev, share_rows, width),
        second_moment.reshape(exp_dev, share_rows, width),
    )
    replicas = lax.axis_size("dp")
    grad_terms = grad_parts[0].reshape(exp_dev, replicas, share_rows, width)
    grad_terms = lax.all_to_all(grad_terms, "dp", split_axis=1, concat_axis=1, tiled=True)
    grad_share = jnp.sum(grad_terms.astype(jnp.float32), axis=1)
    first_new = beta_one * first_moment + (1.0 - beta_one) * grad_share
    second_new = beta_two * second_moment + (1.0 - beta_two) * grad_share * grad_share
    direction = first_new / (jnp.sqrt(second_new) + adam_eps)
    code_first, new_scale_first = quantize(first_new, block_count)
    code_second, new_scale_second = quantize(second_new, block_count)
    return (
        direction,
        jnp.stack([code_first, code_second]),
        jnp.stack([new_scale_first, new_scale_second]),
    )


def iota(shape, dim):
    return lax.broadcasted_iota(jnp.int32, shape, dim)


def dot(a, b, dims=((1,), (0,))):
    return lax.dot_general(a, b, (dims, ((), ())), preferred_element_type=f32)


def pick(rows, chosen, vector):
    return jnp.sum(jnp.where(chosen, vector, 0.0), axis=1, keepdims=True)


def resume_kernel(
    grad_ref,
    m_ref,
    v_ref,
    ms_ref,
    vs_ref,
    map_ref,
    expert_ref,
    row_ref,
    count_ref,
    offset_ref,
    dir_ref,
    codes_ref,
    scales_ref,
    flag_ref,
    old,
    moments,
    relay,
    extra,
    extra_core,
    extra_y,
    extra_z,
    part_core,
    part_y,
    send,
    recv,
    land_own,
    land_plane,
    land_part,
    land_z,
    grads,
    total_grad,
    place,
    late,
    wide_scales,
    load_sem,
    send_sem,
    recv_sem,
    land_ssem,
    land_rsem,
    grad_ssem,
    grad_rsem,
    core_sem,
    y_ssem,
    y_rsem,
    z_ssem,
    z_rsem,
    ready,
):
    d = lax.axis_index("dp")
    e = lax.axis_index("expert")
    z, y, k = lax.div(e, 8), lax.rem(lax.div(e, 2), 4), lax.rem(e, 2)
    share = grads.shape[2]
    owned = 4 * share
    slots = old.shape[0]

    def peer(i):
        pz = lax.rem(z + lax.div(i, 8), 8)
        py = lax.rem(y + lax.rem(lax.div(i, 2), 4), 4)
        pk = lax.rem(k + lax.rem(i, 2), 2)
        return pz * 8 + py * 2 + pk

    def load(p, q):
        source = (m_ref, v_ref)[q // 2]
        return pltpu.make_async_copy(
            source.at[:, pl.ds((q % 2) * 1024 + p * 512, 512)],
            old.at[:, pl.ds(q * 1024 + p * 512, 512)],
            load_sem.at[p * 4 + q],
        )

    for p in range(2):
        for q in range(4):
            load(p, q).start()

    barrier = pltpu.get_barrier_semaphore()

    for i in list(range(1, 8)) + list(range(8, 64, 8)):
        pl.semaphore_signal(barrier, inc=1, device_id=(d, peer(i)), device_id_type=MESH)
    for dx in range(1, 4):
        pl.semaphore_signal(
            barrier, inc=1, device_id=(lax.rem(d + dx, 4), e), device_id_type=MESH
        )

    count = count_ref[...].astype(f32)
    offset = offset_ref[...].astype(f32)
    unit = (iota((16, 16), 0) == iota((16, 16), 1)).astype(bf16)
    columns = (dot(ms_ref[...], unit, ((0,), (0,))), dot(vs_ref[...], unit, ((0,), (0,))))

    row, col = iota((512, 64), 0), iota((512, 64), 1)
    chosen = (row >> 3) == col
    s = (iota((512, 1), 0) & 3).astype(f32)
    source = jnp.where(s < pick(512, chosen, count), pick(512, chosen, offset) + s, -1.0)
    take = (iota((512, slots), 1).astype(f32) == source).astype(bf16)
    low = (iota((512, 256), 0) & 7) < 4

    def dequantize_half(p):
        for q in range(4):
            load(p, q).wait()
        for q in range(4):
            for b in range(4):
                block = (q % 2) * 8 + p * 4 + b
                lanes = slice(q * 1024 + p * 512 + b * 128, q * 1024 + p * 512 + (b + 1) * 128)
                moments[:, lanes] = (
                    old[:, lanes].astype(f32) * columns[q // 2][:, block : block + 1]
                ).astype(bf16)

    def pack(p):
        for c in range(2 * p, 2 * p + 2):
            quarter = [
                dot(take, moments[:, q * 1024 + c * 256 : q * 1024 + (c + 1) * 256])
                for q in range(4)
            ]
            upper = jnp.where(low, quarter[0], quarter[1]).reshape(64, 8, 256)
            lower = jnp.where(low, quarter[2], quarter[3]).reshape(64, 8, 256)
            send[p, :, :, (c % 2) * 256 : (c % 2 + 1) * 256] = jnp.concatenate(
                [upper, lower], axis=1
            ).astype(bf16)

    def remote(source, target, send_s, recv_s, to):
        return pltpu.make_async_remote_copy(
            src_ref=source,
            dst_ref=target,
            send_sem=send_s,
            recv_sem=recv_s,
            device_id=(d, to),
            device_id_type=MESH,
        )

    def land_plane_copy(i):
        to = peer(i)
        return remote(
            land_own.at[pl.ds(pl.multiple_of(lax.rem(to, 8) * 8, 8), 8)],
            land_plane.at[i],
            land_ssem.at[i],
            land_rsem.at[i],
            to,
        )

    def land_z_copy(dz):
        to = lax.rem(z + dz, 8)
        return remote(
            land_part.at[pl.ds(to, 1)],
            land_z.at[pl.ds(dz, 1)],
            land_ssem.at[8 + dz],
            land_rsem.at[8 + dz],
            to * 8 + y * 2 + k,
        )

    urow, ocol = iota((64, 64), 0), iota((64, 64), 1)
    mine = (((urow & 7) << 3) | (urow >> 3)) == ocol
    count_col = pick(64, mine, count)
    offset_col = pick(64, mine, offset)
    lane = iota((64, slots), 1).astype(f32)
    held = jnp.logical_and(lane >= offset_col, lane < offset_col + count_col)
    rank = iota((1, slots), 1).astype(f32) - jnp.sum(
        jnp.where(held, offset_col, 0.0), axis=0, keepdims=True
    )
    old_place = iota((256, slots), 0) == expert_ref[...]
    mapped = dot(
        jnp.broadcast_to(map_ref[...].astype(f32), (8, 256)).astype(bf16), old_place.astype(bf16)
    )[0:1]
    land = (mapped - 4.0 * jnp.floor(mapped * 0.25)) * float(share) + row_ref[...].astype(f32) + 1.0
    held_land = jnp.where(held, land, 0.0).astype(bf16)
    at_rank = (iota((128, slots), 0).astype(f32) == rank).astype(bf16)
    targets = dot(held_land, at_rank, ((1,), (1,)))
    slot, lane = iota((128, 384), 0), iota((128, 384), 1)
    first = jnp.logical_and(slot < BASE, lane == e * BASE + slot)
    later = jnp.logical_and(slot >= BASE, lane == 256 + slot - BASE)
    keep = jnp.where(jnp.logical_or(first, later), 1.0, 0.0).astype(bf16)
    tell = (iota((64, 384), 0) + 320 == iota((64, 384), 1)).astype(bf16)
    heavy = jnp.broadcast_to((count > float(BASE)).astype(f32), (64, 64)).astype(bf16)
    land_own[...] = dot(targets.astype(bf16), keep) + dot(heavy, tell)

    dequantize_half(0)
    pl.semaphore_wait(barrier, 17)
    for i in range(1, 8):
        pl.semaphore_signal(ready, inc=1, device_id=(d, peer(i)), device_id_type=MESH)
    for i in range(1, 8):
        land_plane_copy(i).start()
    pack(0)
    pl.semaphore_wait(ready, 7)

    def grad_copy(dx):
        to = lax.rem(d + dx, 4)
        return pltpu.make_async_remote_copy(
            src_ref=grad_ref.at[0, :, pl.ds(pl.multiple_of(to * share, 16), share), :],
            dst_ref=grads.at[dx],
            send_sem=grad_ssem.at[dx],
            recv_sem=grad_rsem.at[dx],
            device_id=(to, e),
            device_id_type=MESH,
        )

    own_grad = pltpu.make_async_copy(
        grad_ref.at[0, :, pl.ds(pl.multiple_of(d * share, 16), share), :], grads.at[0], grad_ssem.at[0]
    )

    columns_of = [lax.rem(y + j // 2, 4) * 2 + lax.rem(k + j % 2, 2) for j in range(8)]

    def start_main(p, low, high):
        def plane(dz, carry):
            base = lax.rem(z + dz, 8) * 8
            for j in range(8):
                to = base + columns_of[j]
                remote(send.at[p, to], recv.at[p, e], send_sem.at[p], recv_sem.at[p], to).start()
            return carry

        lax.fori_loop(low, high, plane, 0)

    def start_own_plane(p):
        for j in range(1, 8):
            to = z * 8 + columns_of[j]
            remote(send.at[p, to], recv.at[p, e], send_sem.at[p], recv_sem.at[p], to).start()

    def wait_main(p):
        all_others = pl.ds(0, 63)
        remote(
            send.at[p, all_others], recv.at[p, all_others], send_sem.at[p], recv_sem.at[p], peer(1)
        ).wait()

    for dx in range(1, 4):
        grad_copy(dx).start()
    own_grad.start()
    start_main(0, 1, 8)
    start_own_plane(0)
    for i in range(1, 8):
        land_plane_copy(i).wait()
    land_plane[0] = land_own[pl.ds(pl.multiple_of(lax.rem(e, 8) * 8, 8), 8), :]
    land_part[...] = jnp.sum(land_plane[...], axis=0)
    for dz in range(1, 8):
        land_z_copy(dz).start()
    land_z[pl.ds(0, 1), :] = land_part[pl.ds(z, 1), :]
    recv[0, e] = send[0, e]

    dequantize_half(1)
    row, col = iota((64 * EXTRA, 64), 0), iota((64 * EXTRA, 64), 1)
    u = row & 63
    owner = ((u & 7) << 3) | (((u >> 3) & 3) << 1) | (u >> 5)
    chosen = owner == col
    s = (iota((64 * EXTRA, 1), 0) >> 6).astype(f32) + float(BASE)
    source = jnp.where(
        s < pick(64 * EXTRA, chosen, count), pick(64 * EXTRA, chosen, offset) + s, -1.0
    )
    take_extra = (iota((64 * EXTRA, slots), 1).astype(f32) == source).astype(bf16)
    for c in range(8):
        rows = dot(take_extra, moments[:, c * 512 : (c + 1) * 512])
        for s_i in range(EXTRA):
            for q in range(4):
                relay[pl.ds(s_i * 32 + c * 4 + q, 64, stride=32 * EXTRA), :] = rows[
                    s_i * 64 : (s_i + 1) * 64, q * 128 : (q + 1) * 128
                ]

    def narrow(u, carry):
        extra[u] = relay[pl.ds(pl.multiple_of(u * 32 * EXTRA, 32), 32 * EXTRA), :].astype(bf16)
        return carry

    lax.fori_loop(0, 64, narrow, 0)

    core_copy = pltpu.make_async_remote_copy(
        src_ref=extra.at[pl.ds((1 - k) * 32, 32)],
        dst_ref=extra_core,
        send_sem=core_sem.at[0],
        recv_sem=core_sem.at[1],
        device_id=(d, peer(1)),
        device_id_type=MESH,
    )
    core_copy.start()
    pack(1)
    core_copy.wait()

    def add_core(g, carry):
        part_core[g] = extra[k * 32 + g] + extra_core[g]
        return carry

    lax.fori_loop(0, 32, add_core, 0)

    def y_copy(dy):
        to = lax.rem(y + dy, 4)
        return pltpu.make_async_remote_copy(
            src_ref=part_core.at[pl.ds(to * 8, 8)],
            dst_ref=extra_y.at[dy - 1],
            send_sem=y_ssem.at[dy - 1],
            recv_sem=y_rsem.at[dy - 1],
            device_id=(d, z * 8 + to * 2 + k),
            device_id_type=MESH,
        )

    def z_copy(dz):
        to = lax.rem(z + dz, 8)
        return pltpu.make_async_remote_copy(
            src_ref=part_y.at[to],
            dst_ref=extra_z.at[dz - 1],
            send_sem=z_ssem.at[dz - 1],
            recv_sem=z_rsem.at[dz - 1],
            device_id=(d, to * 8 + y * 2 + k),
            device_id_type=MESH,
        )

    for dy in range(1, 4):
        y_copy(dy).start()
    start_main(1, 3, 6)

    for dy in range(1, 4):
        y_copy(dy).wait()

    def add_y(g, carry):
        part_y[g] = part_core[y * 8 + g] + (extra_y[0, g] + (extra_y[1, g] + extra_y[2, g]))
        return carry

    lax.fori_loop(0, 8, add_y, 0)
    for dz in range(1, 8):
        z_copy(dz).start()
    start_main(1, 6, 8)
    start_main(1, 1, 3)
    start_own_plane(1)

    recv[1, e] = send[1, e]

    own_grad.wait()
    for dx in range(1, 4):
        grad_copy(dx).wait()
    for ex in range(4):
        total_grad[ex] = (grads[0, ex].astype(f32) + grads[1, ex].astype(f32)) + (
            grads[2, ex].astype(f32) + grads[3, ex].astype(f32)
        )

    for dz in range(1, 8):
        land_z_copy(dz).wait()
    landing = jnp.sum(land_z[...], axis=0, keepdims=True)
    flag_ref[0] = jnp.max(landing[:, 256:] * (iota((1, 128), 1) >= 64).astype(f32)).astype(jnp.int32)
    near, lane = iota((256, 1024), 0), iota((256, 1024), 1)
    spread = jnp.logical_and((near >> 2) == (lane >> 4), (near & 3) == (lane & 3))
    goal = dot(
        jnp.broadcast_to(landing[:, :256], (8, 256)).astype(bf16),
        jnp.where(spread, 1.0, 0.0).astype(bf16),
    )[0:1]
    lane = iota((1, 1024), 1)
    hit = iota((owned, 1024), 0).astype(f32) + 1.0 == goal
    for q in range(4):
        place[q * owned : (q + 1) * owned, :] = jnp.where(
            jnp.logical_and(hit, ((lane >> 2) & 3) == q), 1.0, 0.0
        ).astype(bf16)
    late_hit = jnp.logical_and(
        iota((owned, 128), 0).astype(f32) + 1.0 == landing[:, 256:], iota((owned, 128), 1) < EXTRA
    )
    late_place = jnp.where(late_hit, 1.0, 0.0).astype(bf16)[:, :16]

    for dz in range(1, 8):
        z_copy(dz).wait()
    late[...] = jnp.zeros_like(late)
    total = part_y[z].astype(f32)
    for dz in range(1, 8):
        total = total + extra_z[dz - 1].astype(f32)
    late[: EXTRA * 32, :] = total

    def unpack(p):
        for c in range(2):
            arrived = dot(
                place[...], recv[p, :, :, c * 256 : (c + 1) * 256].reshape(1024, 256)
            )
            for q in range(4):
                for b in range(2):
                    block = p * 4 + c * 2 + b
                    rest = late[pl.ds(q * 8 + block, 16, stride=32), :].astype(bf16)
                    relay[(q * 8 + block) * owned : (q * 8 + block + 1) * owned, :] = arrived[
                        q * owned : (q + 1) * owned, b * 128 : (b + 1) * 128
                    ] + dot(late_place, rest)

    def update(p):
        def one(ex, carry):
            scale_lane = iota((share, 16), 1)
            m_scales = wide_scales[0, ex]
            v_scales = wide_scales[1, ex]
            for b in [h * 8 + p * 4 + i for h in range(2) for i in range(4)]:
                at = pl.ds(pl.multiple_of(ex * share, 16) + b * owned, share)
                at_v = pl.ds(pl.multiple_of(ex * share, 16) + (16 + b) * owned, share)
                out = slice(b * 128, (b + 1) * 128)
                g = total_grad[ex, :, out]
                m = beta_one * relay[at, :] + (1.0 - beta_one) * g
                v = beta_two * relay[at_v, :] + (1.0 - beta_two) * g * g
                dir_ref[ex, :, out] = m / (jnp.sqrt(v) + adam_eps)
                m_scale = (jnp.max(jnp.abs(m), axis=1, keepdims=True) + scale_eps).astype(bf16)
                v_scale = (jnp.max(jnp.abs(v), axis=1, keepdims=True) + scale_eps).astype(bf16)
                m_wide, v_wide = m_scale.astype(f32), v_scale.astype(f32)
                codes_ref[0, ex, :, out] = (m * (1.0 / m_wide)).astype(bf16)
                codes_ref[1, ex, :, out] = (v * (1.0 / v_wide)).astype(bf16)
                m_scales = jnp.where(scale_lane == b, m_wide, m_scales)
                v_scales = jnp.where(scale_lane == b, v_wide, v_scales)
            wide_scales[0, ex] = m_scales
            wide_scales[1, ex] = v_scales
            return carry

        lax.fori_loop(0, 4, one, 0)

    wide_scales[...] = jnp.zeros_like(wide_scales)
    for p in range(2):
        wait_main(p)
        unpack(p)
        update(p)
    turn = (iota((share, share), 0) == iota((share, share), 1)).astype(bf16)
    for part in range(2):
        for ex in range(4):
            scales_ref[part, ex] = dot(
                wide_scales[part, ex].astype(bf16), turn, ((0,), (0,))
            ).astype(bf16)


def hand_on_kernel(dir_ref, codes_ref, scales_ref, dir_to, codes_to, scales_to, sem):
    copies = [pltpu.make_async_copy(scales_ref, scales_to, sem.at[12])]
    for ex in range(4):
        copies.append(pltpu.make_async_copy(dir_ref.at[ex], dir_to.at[ex], sem.at[ex]))
        for part in range(2):
            copies.append(
                pltpu.make_async_copy(
                    codes_ref.at[part, ex], codes_to.at[part, ex], sem.at[4 + part * 4 + ex]
                )
            )
    for copy in copies:
        copy.start()
    for copy in copies:
        copy.wait()


def hand_on(*results):
    return tuple(
        pl.pallas_call(
            hand_on_kernel,
            out_shape=tuple(jax.ShapeDtypeStruct(r.shape, r.dtype) for r in results),
            in_specs=[pl.BlockSpec(memory_space=pltpu.VMEM)] * 3,
            out_specs=(pl.BlockSpec(memory_space=pl.ANY),) * 3,
            scratch_shapes=[pltpu.SemaphoreType.DMA((13,))],
            compiler_params=pltpu.CompilerParams(vmem_limit_bytes=8 * 2**20),
            name="hand_on",
        )(*[pltpu.with_memory_space_constraint(r, pltpu.VMEM) for r in results])
    )


def exchange(grad_parts, m_codes, v_codes, m_scale, v_scale, expert_map, slot_expert, slot_row, count, offset):
    slots, width, blocks = m_codes.shape[2], m_codes.shape[3], m_scale.shape[3]
    share = grad_parts.shape[2] // 4
    owned = 4 * share
    vmem = pl.BlockSpec(memory_space=pltpu.VMEM)
    hbm = pl.BlockSpec(memory_space=pl.ANY)
    chunk = 32 * EXTRA
    direction, codes, scales, heavy = pl.pallas_call(
        resume_kernel,
        out_shape=(
            pltpu.VMEM((4, share, width), f32),
            pltpu.VMEM((2, 4, share, width), bf16),
            pltpu.VMEM((2, 4, blocks, share), bf16),
            jax.ShapeDtypeStruct((1,), jnp.int32),
        ),
        in_specs=[hbm] * 3 + [vmem] * 7,
        out_specs=(vmem, vmem, vmem, pl.BlockSpec(memory_space=pltpu.SMEM)),
        scratch_shapes=[
            pltpu.VMEM((slots, 2 * width), bf16),
            pltpu.VMEM((slots, 2 * width), bf16),
            pltpu.VMEM((64 * chunk, 128), f32),
            pltpu.VMEM((64, chunk, 128), bf16),
            pltpu.VMEM((32, chunk, 128), bf16),
            pltpu.VMEM((3, 8, chunk, 128), bf16),
            pltpu.VMEM((7, chunk, 128), bf16),
            pltpu.VMEM((32, chunk, 128), bf16),
            pltpu.VMEM((8, chunk, 128), bf16),
            pltpu.VMEM((2, 64, 16, 512), bf16),
            pltpu.VMEM((2, 64, 16, 512), bf16),
            pltpu.VMEM((64, 384), f32),
            pltpu.VMEM((8, 8, 384), f32),
            pltpu.VMEM((8, 384), f32),
            pltpu.VMEM((8, 384), f32),
            pltpu.VMEM((4, 4, share, width), bf16),
            pltpu.VMEM((4, share, width), f32),
            pltpu.VMEM((4 * owned, 1024), bf16),
            pltpu.VMEM((16 * 32, 128), f32),
            pltpu.VMEM((2, 4, share, 16), f32),
            pltpu.SemaphoreType.DMA((8,)),
            pltpu.SemaphoreType.DMA((2,)),
            pltpu.SemaphoreType.DMA((2,)),
            pltpu.SemaphoreType.DMA((16,)),
            pltpu.SemaphoreType.DMA((16,)),
            pltpu.SemaphoreType.DMA((4,)),
            pltpu.SemaphoreType.DMA((4,)),
            pltpu.SemaphoreType.DMA((2,)),
            pltpu.SemaphoreType.DMA((3,)),
            pltpu.SemaphoreType.DMA((3,)),
            pltpu.SemaphoreType.DMA((7,)),
            pltpu.SemaphoreType.DMA((7,)),
            pltpu.SemaphoreType.REGULAR,
        ],
        compiler_params=pltpu.CompilerParams(
            collective_id=0, has_side_effects=True, vmem_limit_bytes=VMEM_MIB * 2**20
        ),
        name="resume",
    )(
        grad_parts,
        m_codes[0, 0],
        v_codes[0, 0],
        m_scale[0, 0].T,
        v_scale[0, 0].T,
        expert_map.reshape(1, -1),
        slot_expert,
        slot_row,
        count,
        offset,
    )
    return direction, codes, scales, heavy


def per_device(*args):
    direction, codes, scales, heavy = exchange(*args)

    def padded():
        direction, codes, scales = padded_exchange(*args)
        return direction, codes, jnp.swapaxes(scales, 2, 3)

    direction, codes, scales = lax.cond(
        heavy[0] < 2, lambda: hand_on(direction, codes, scales), padded
    )
    return direction, codes, jnp.swapaxes(scales, 2, 3)


def solution(mesh):
    in_specs = (
        P("dp", "expert", None, None),
        P("dp", "expert", None, None),
        P("dp", "expert", None, None),
        P("dp", "expert", None, None),
        P("dp", "expert", None, None),
        P(),
        P("expert", None),
        P("expert", None),
        P("expert", None),
        P("expert", None),
    )
    out_specs = (
        P("expert", "dp", None),
        P(None, "expert", "dp", None),
        P(None, "expert", "dp", None),
    )
    return jax.shard_map(
        per_device, mesh=mesh, in_specs=in_specs, out_specs=out_specs, check_vma=False
    )
```

```python
import functools

import jax
import jax.numpy as jnp
from jax import lax
from jax.experimental import pallas as pl
from jax.experimental.pallas import tpu as pltpu
from jax.sharding import PartitionSpec as P

beta_one = 0.9
beta_two = 0.95
adam_eps = 1e-08
scale_eps = 1e-06

MESH = pl.DeviceIdType.MESH
f32 = jnp.float32
bf16 = jnp.bfloat16
BASE = 4
EXTRA = 5
VMEM_MIB = 44


def dequantize(code_array, block_scale):
    full_shape = code_array.shape
    blocks = code_array.astype(jnp.float32).reshape(
        full_shape[:-1] + (block_scale.shape[-1], full_shape[-1] // block_scale.shape[-1])
    )
    return (blocks * block_scale.astype(jnp.float32)[..., None]).reshape(full_shape)


def quantize(values, block_count):
    full_shape = values.shape
    blocks = values.reshape(full_shape[:-1] + (block_count, full_shape[-1] // block_count))
    block_scale = (jnp.max(jnp.abs(blocks), axis=-1) + scale_eps).astype(jnp.bfloat16)
    code_array = (blocks / block_scale.astype(jnp.float32)[..., None]).astype(jnp.bfloat16)
    return (code_array.reshape(full_shape), block_scale)


def padded_exchange(
    grad_parts,
    old_m_codes,
    old_v_codes,
    old_m_scale,
    old_v_scale,
    expert_map,
    slot_expert,
    slot_row,
    peer_count,
    peer_offset,
):
    owners = lax.axis_size("expert")
    codes_first = old_m_codes[0, 0]
    codes_second = old_v_codes[0, 0]
    scale_first = old_m_scale[0, 0]
    scale_second = old_v_scale[0, 0]
    slot_total = codes_first.shape[0]
    width = codes_first.shape[1]
    block_count = scale_first.shape[1]
    per_peer = slot_total // owners
    exp_dev = grad_parts.shape[1]
    share_rows = grad_parts.shape[2] // lax.axis_size("dp")
    owned_rows = exp_dev * share_rows
    send_counts = peer_count[0]
    offsets = peer_offset[0]
    slot_place = jnp.arange(per_peer, dtype=jnp.int32)[None, :]
    picked = (offsets[:, None] + slot_place).reshape(-1)
    new_expert = expert_map[slot_expert[0]]
    local_all = new_expert % exp_dev * share_rows + slot_row[0]
    usable = slot_place < send_counts[:, None]
    targets = jnp.where(usable, local_all[picked].reshape(owners, per_peer), -1)
    arrived_targets = lax.all_to_all(targets, "expert", split_axis=0, concat_axis=0, tiled=True)
    sent_first = dequantize(codes_first[picked], scale_first[picked]).reshape(
        owners, per_peer, width
    )
    sent_second = dequantize(codes_second[picked], scale_second[picked]).reshape(
        owners, per_peer, width
    )
    first_rows = lax.all_to_all(
        sent_first.astype(jnp.bfloat16), "expert", split_axis=0, concat_axis=0, tiled=True
    ).astype(sent_first.dtype)
    second_rows = lax.all_to_all(
        sent_second.astype(jnp.bfloat16), "expert", split_axis=0, concat_axis=0, tiled=True
    ).astype(sent_second.dtype)
    flat_targets = arrived_targets.reshape(-1)
    landing = jnp.where(flat_targets >= 0, flat_targets, owned_rows)
    first_moment = (
        jnp.zeros((owned_rows, width), jnp.float32)
        .at[landing]
        .set(first_rows.reshape(-1, width), mode="drop")
    )
    second_moment = (
        jnp.zeros((owned_rows, width), jnp.float32)
        .at[landing]
        .set(second_rows.reshape(-1, width), mode="drop")
    )
    first_moment, second_moment = (
        first_moment.reshape(exp_dev, share_rows, width),
        second_moment.reshape(exp_dev, share_rows, width),
    )
    replicas = lax.axis_size("dp")
    grad_terms = grad_parts[0].reshape(exp_dev, replicas, share_rows, width)
    grad_terms = lax.all_to_all(grad_terms, "dp", split_axis=1, concat_axis=1, tiled=True)
    grad_share = jnp.sum(grad_terms.astype(jnp.float32), axis=1)
    first_new = beta_one * first_moment + (1.0 - beta_one) * grad_share
    second_new = beta_two * second_moment + (1.0 - beta_two) * grad_share * grad_share
    direction = first_new / (jnp.sqrt(second_new) + adam_eps)
    code_first, new_scale_first = quantize(first_new, block_count)
    code_second, new_scale_second = quantize(second_new, block_count)
    return (
        direction,
        jnp.stack([code_first, code_second]),
        jnp.stack([new_scale_first, new_scale_second]),
    )


def iota(shape, dim):
    return lax.broadcasted_iota(jnp.int32, shape, dim)


def dot(a, b, dims=((1,), (0,))):
    return lax.dot_general(a, b, (dims, ((), ())), preferred_element_type=f32)


def pick(rows, chosen, vector):
    return jnp.sum(jnp.where(chosen, vector, 0.0), axis=1, keepdims=True)


def resume_kernel(
    grad_ref,
    m_ref,
    v_ref,
    ms_ref,
    vs_ref,
    map_ref,
    expert_ref,
    row_ref,
    count_ref,
    offset_ref,
    dir_ref,
    codes_ref,
    scales_ref,
    flag_ref,
    old,
    moments,
    relay,
    extra,
    extra_core,
    extra_y,
    extra_z,
    part_core,
    part_y,
    send,
    recv,
    land_own,
    land_plane,
    land_part,
    land_z,
    grads,
    total_grad,
    place,
    late,
    wide_scales,
    load_sem,
    send_sem,
    recv_sem,
    land_ssem,
    land_rsem,
    grad_ssem,
    grad_rsem,
    core_sem,
    y_ssem,
    y_rsem,
    z_ssem,
    z_rsem,
    ready,
):
    d = lax.axis_index("dp")
    e = lax.axis_index("expert")
    z, y, k = lax.div(e, 8), lax.rem(lax.div(e, 2), 4), lax.rem(e, 2)
    share = grads.shape[2]
    owned = 4 * share
    slots = old.shape[0]

    def peer(i):
        pz = lax.rem(z + lax.div(i, 8), 8)
        py = lax.rem(y + lax.rem(lax.div(i, 2), 4), 4)
        pk = lax.rem(k + lax.rem(i, 2), 2)
        return pz * 8 + py * 2 + pk

    def load(p, q):
        source = (m_ref, v_ref)[q // 2]
        return pltpu.make_async_copy(
            source.at[:, pl.ds((q % 2) * 1024 + p * 512, 512)],
            old.at[:, pl.ds(q * 1024 + p * 512, 512)],
            load_sem.at[p * 4 + q],
        )

    for p in range(2):
        for q in range(4):
            load(p, q).start()

    barrier = pltpu.get_barrier_semaphore()

    for i in list(range(1, 8)) + list(range(8, 64, 8)):
        pl.semaphore_signal(barrier, inc=1, device_id=(d, peer(i)), device_id_type=MESH)
    for dx in range(1, 4):
        pl.semaphore_signal(
            barrier, inc=1, device_id=(lax.rem(d + dx, 4), e), device_id_type=MESH
        )

    count = count_ref[...].astype(f32)
    offset = offset_ref[...].astype(f32)
    unit = (iota((16, 16), 0) == iota((16, 16), 1)).astype(bf16)
    columns = (dot(ms_ref[...], unit, ((0,), (0,))), dot(vs_ref[...], unit, ((0,), (0,))))

    row, col = iota((512, 64), 0), iota((512, 64), 1)
    chosen = (row >> 3) == col
    s = (iota((512, 1), 0) & 3).astype(f32)
    source = jnp.where(s < pick(512, chosen, count), pick(512, chosen, offset) + s, -1.0)
    take = (iota((512, slots), 1).astype(f32) == source).astype(bf16)
    low = (iota((512, 256), 0) & 7) < 4

    def dequantize_half(p):
        for q in range(4):
            load(p, q).wait()
        for q in range(4):
            for b in range(4):
                block = (q % 2) * 8 + p * 4 + b
                lanes = slice(q * 1024 + p * 512 + b * 128, q * 1024 + p * 512 + (b + 1) * 128)
                moments[:, lanes] = (
                    old[:, lanes].astype(f32) * columns[q // 2][:, block : block + 1]
                ).astype(bf16)

    def pack(p):
        for c in range(2 * p, 2 * p + 2):
            quarter = [
                dot(take, moments[:, q * 1024 + c * 256 : q * 1024 + (c + 1) * 256])
                for q in range(4)
            ]
            upper = jnp.where(low, quarter[0], quarter[1]).reshape(64, 8, 256)
            lower = jnp.where(low, quarter[2], quarter[3]).reshape(64, 8, 256)
            send[p, :, :, (c % 2) * 256 : (c % 2 + 1) * 256] = jnp.concatenate(
                [upper, lower], axis=1
            ).astype(bf16)

    def remote(source, target, send_s, recv_s, to):
        return pltpu.make_async_remote_copy(
            src_ref=source,
            dst_ref=target,
            send_sem=send_s,
            recv_sem=recv_s,
            device_id=(d, to),
            device_id_type=MESH,
        )

    def land_plane_copy(i):
        to = peer(i)
        return remote(
            land_own.at[pl.ds(pl.multiple_of(lax.rem(to, 8) * 8, 8), 8)],
            land_plane.at[i],
            land_ssem.at[i],
            land_rsem.at[i],
            to,
        )

    def land_z_copy(dz):
        to = lax.rem(z + dz, 8)
        return remote(
            land_part.at[pl.ds(to, 1)],
            land_z.at[pl.ds(dz, 1)],
            land_ssem.at[8 + dz],
            land_rsem.at[8 + dz],
            to * 8 + y * 2 + k,
        )

    urow, ocol = iota((64, 64), 0), iota((64, 64), 1)
    mine = (((urow & 7) << 3) | (urow >> 3)) == ocol
    count_col = pick(64, mine, count)
    offset_col = pick(64, mine, offset)
    lane = iota((64, slots), 1).astype(f32)
    held = jnp.logical_and(lane >= offset_col, lane < offset_col + count_col)
    rank = iota((1, slots), 1).astype(f32) - jnp.sum(
        jnp.where(held, offset_col, 0.0), axis=0, keepdims=True
    )
    old_place = iota((256, slots), 0) == expert_ref[...]
    mapped = dot(
        jnp.broadcast_to(map_ref[...].astype(f32), (8, 256)).astype(bf16), old_place.astype(bf16)
    )[0:1]
    land = (mapped - 4.0 * jnp.floor(mapped * 0.25)) * float(share) + row_ref[...].astype(f32) + 1.0
    held_land = jnp.where(held, land, 0.0).astype(bf16)
    at_rank = (iota((128, slots), 0).astype(f32) == rank).astype(bf16)
    targets = dot(held_land, at_rank, ((1,), (1,)))
    slot, lane = iota((128, 384), 0), iota((128, 384), 1)
    first = jnp.logical_and(slot < BASE, lane == e * BASE + slot)
    later = jnp.logical_and(slot >= BASE, lane == 256 + slot - BASE)
    keep = jnp.where(jnp.logical_or(first, later), 1.0, 0.0).astype(bf16)
    tell = (iota((64, 384), 0) + 320 == iota((64, 384), 1)).astype(bf16)
    heavy = jnp.broadcast_to((count > float(BASE)).astype(f32), (64, 64)).astype(bf16)
    land_own[...] = dot(targets.astype(bf16), keep) + dot(heavy, tell)

    dequantize_half(0)
    pl.semaphore_wait(barrier, 17)
    for i in range(1, 8):
        pl.semaphore_signal(ready, inc=1, device_id=(d, peer(i)), device_id_type=MESH)
    for i in range(1, 8):
        land_plane_copy(i).start()
    pack(0)
    pl.semaphore_wait(ready, 7)

    def grad_copy(dx):
        to = lax.rem(d + dx, 4)
        return pltpu.make_async_remote_copy(
            src_ref=grad_ref.at[0, :, pl.ds(pl.multiple_of(to * share, 16), share), :],
            dst_ref=grads.at[dx],
            send_sem=grad_ssem.at[dx],
            recv_sem=grad_rsem.at[dx],
            device_id=(to, e),
            device_id_type=MESH,
        )

    own_grad = pltpu.make_async_copy(
        grad_ref.at[0, :, pl.ds(pl.multiple_of(d * share, 16), share), :], grads.at[0], grad_ssem.at[0]
    )

    columns_of = [lax.rem(y + j // 2, 4) * 2 + lax.rem(k + j % 2, 2) for j in range(8)]

    def start_main(p, low, high):
        def plane(dz, carry):
            base = lax.rem(z + dz, 8) * 8
            for j in range(8):
                to = base + columns_of[j]
                remote(send.at[p, to], recv.at[p, e], send_sem.at[p], recv_sem.at[p], to).start()
            return carry

        lax.fori_loop(low, high, plane, 0)

    def start_own_plane(p):
        for j in range(1, 8):
            to = z * 8 + columns_of[j]
            remote(send.at[p, to], recv.at[p, e], send_sem.at[p], recv_sem.at[p], to).start()

    def wait_main(p):
        all_others = pl.ds(0, 63)
        remote(
            send.at[p, all_others], recv.at[p, all_others], send_sem.at[p], recv_sem.at[p], peer(1)
        ).wait()

    for dx in range(1, 4):
        grad_copy(dx).start()
    own_grad.start()
    start_main(0, 1, 8)
    start_own_plane(0)
    for i in range(1, 8):
        land_plane_copy(i).wait()
    land_plane[0] = land_own[pl.ds(pl.multiple_of(lax.rem(e, 8) * 8, 8), 8), :]
    land_part[...] = jnp.sum(land_plane[...], axis=0)
    for dz in range(1, 8):
        land_z_copy(dz).start()
    land_z[pl.ds(0, 1), :] = land_part[pl.ds(z, 1), :]
    recv[0, e] = send[0, e]

    dequantize_half(1)
    row, col = iota((64 * EXTRA, 64), 0), iota((64 * EXTRA, 64), 1)
    u = row & 63
    owner = ((u & 7) << 3) | (((u >> 3) & 3) << 1) | (u >> 5)
    chosen = owner == col
    s = (iota((64 * EXTRA, 1), 0) >> 6).astype(f32) + float(BASE)
    source = jnp.where(
        s < pick(64 * EXTRA, chosen, count), pick(64 * EXTRA, chosen, offset) + s, -1.0
    )
    take_extra = (iota((64 * EXTRA, slots), 1).astype(f32) == source).astype(bf16)
    for c in range(8):
        rows = dot(take_extra, moments[:, c * 512 : (c + 1) * 512])
        for s_i in range(EXTRA):
            for q in range(4):
                relay[pl.ds(s_i * 32 + c * 4 + q, 64, stride=32 * EXTRA), :] = rows[
                    s_i * 64 : (s_i + 1) * 64, q * 128 : (q + 1) * 128
                ]

    def narrow(u, carry):
        extra[u] = relay[pl.ds(pl.multiple_of(u * 32 * EXTRA, 32), 32 * EXTRA), :].astype(bf16)
        return carry

    lax.fori_loop(0, 64, narrow, 0)

    core_copy = pltpu.make_async_remote_copy(
        src_ref=extra.at[pl.ds((1 - k) * 32, 32)],
        dst_ref=extra_core,
        send_sem=core_sem.at[0],
        recv_sem=core_sem.at[1],
        device_id=(d, peer(1)),
        device_id_type=MESH,
    )
    core_copy.start()
    pack(1)
    core_copy.wait()

    def add_core(g, carry):
        part_core[g] = extra[k * 32 + g] + extra_core[g]
        return carry

    lax.fori_loop(0, 32, add_core, 0)

    def y_copy(dy):
        to = lax.rem(y + dy, 4)
        return pltpu.make_async_remote_copy(
            src_ref=part_core.at[pl.ds(to * 8, 8)],
            dst_ref=extra_y.at[dy - 1],
            send_sem=y_ssem.at[dy - 1],
            recv_sem=y_rsem.at[dy - 1],
            device_id=(d, z * 8 + to * 2 + k),
            device_id_type=MESH,
        )

    def z_copy(dz):
        to = lax.rem(z + dz, 8)
        return pltpu.make_async_remote_copy(
            src_ref=part_y.at[to],
            dst_ref=extra_z.at[dz - 1],
            send_sem=z_ssem.at[dz - 1],
            recv_sem=z_rsem.at[dz - 1],
            device_id=(d, to * 8 + y * 2 + k),
            device_id_type=MESH,
        )

    for dy in range(1, 4):
        y_copy(dy).start()
    start_main(1, 3, 6)

    for dy in range(1, 4):
        y_copy(dy).wait()

    def add_y(g, carry):
        part_y[g] = part_core[y * 8 + g] + (extra_y[0, g] + (extra_y[1, g] + extra_y[2, g]))
        return carry

    lax.fori_loop(0, 8, add_y, 0)
    for dz in range(1, 8):
        z_copy(dz).start()
    start_main(1, 6, 8)
    start_main(1, 1, 3)
    start_own_plane(1)

    recv[1, e] = send[1, e]

    own_grad.wait()
    for dx in range(1, 4):
        grad_copy(dx).wait()
    for ex in range(4):
        total_grad[ex] = (grads[0, ex].astype(f32) + grads[1, ex].astype(f32)) + (
            grads[2, ex].astype(f32) + grads[3, ex].astype(f32)
        )

    for dz in range(1, 8):
        land_z_copy(dz).wait()
    landing = jnp.sum(land_z[...], axis=0, keepdims=True)
    flag_ref[0] = jnp.max(landing[:, 256:] * (iota((1, 128), 1) >= 64).astype(f32)).astype(jnp.int32)
    near, lane = iota((256, 1024), 0), iota((256, 1024), 1)
    spread = jnp.logical_and((near >> 2) == (lane >> 4), (near & 3) == (lane & 3))
    goal = dot(
        jnp.broadcast_to(landing[:, :256], (8, 256)).astype(bf16),
        jnp.where(spread, 1.0, 0.0).astype(bf16),
    )[0:1]
    lane = iota((1, 1024), 1)
    hit = iota((owned, 1024), 0).astype(f32) + 1.0 == goal
    for q in range(4):
        place[q * owned : (q + 1) * owned, :] = jnp.where(
            jnp.logical_and(hit, ((lane >> 2) & 3) == q), 1.0, 0.0
        ).astype(bf16)
    late_hit = jnp.logical_and(
        iota((owned, 128), 0).astype(f32) + 1.0 == landing[:, 256:], iota((owned, 128), 1) < EXTRA
    )
    late_place = jnp.where(late_hit, 1.0, 0.0).astype(bf16)[:, :16]

    for dz in range(1, 8):
        z_copy(dz).wait()
    late[...] = jnp.zeros_like(late)
    total = part_y[z].astype(f32)
    for dz in range(1, 8):
        total = total + extra_z[dz - 1].astype(f32)
    late[: EXTRA * 32, :] = total

    def unpack_late(p):
        for q in range(4):
            for i in range(4):
                block = q * 8 + p * 4 + i
                rest = late[pl.ds(block, 16, stride=32), :].astype(bf16)
                relay[block * owned : (block + 1) * owned, :] = dot(late_place, rest)

    def unpack(p):
        for c in range(2):
            arrived = dot(
                place[...], recv[p, :, :, c * 256 : (c + 1) * 256].reshape(1024, 256)
            )
            for q in range(4):
                for b in range(2):
                    block = q * 8 + p * 4 + c * 2 + b
                    rows = slice(block * owned, (block + 1) * owned)
                    relay[rows, :] = relay[rows, :] + arrived[
                        q * owned : (q + 1) * owned, b * 128 : (b + 1) * 128
                    ]

    def update(p):
        def one(ex, carry):
            scale_lane = iota((share, 16), 1)
            m_scales = wide_scales[0, ex]
            v_scales = wide_scales[1, ex]
            for b in [h * 8 + p * 4 + i for h in range(2) for i in range(4)]:
                at = pl.ds(pl.multiple_of(ex * share, 16) + b * owned, share)
                at_v = pl.ds(pl.multiple_of(ex * share, 16) + (16 + b) * owned, share)
                out = slice(b * 128, (b + 1) * 128)
                g = total_grad[ex, :, out]
                m = beta_one * relay[at, :] + (1.0 - beta_one) * g
                v = beta_two * relay[at_v, :] + (1.0 - beta_two) * g * g
                dir_ref[ex, :, out] = m / (jnp.sqrt(v) + adam_eps)
                m_scale = (jnp.max(jnp.abs(m), axis=1, keepdims=True) + scale_eps).astype(bf16)
                v_scale = (jnp.max(jnp.abs(v), axis=1, keepdims=True) + scale_eps).astype(bf16)
                m_wide, v_wide = m_scale.astype(f32), v_scale.astype(f32)
                codes_ref[0, ex, :, out] = (m * (1.0 / m_wide)).astype(bf16)
                codes_ref[1, ex, :, out] = (v * (1.0 / v_wide)).astype(bf16)
                m_scales = jnp.where(scale_lane == b, m_wide, m_scales)
                v_scales = jnp.where(scale_lane == b, v_wide, v_scales)
            wide_scales[0, ex] = m_scales
            wide_scales[1, ex] = v_scales
            return carry

        lax.fori_loop(0, 4, one, 0)

    wide_scales[...] = jnp.zeros_like(wide_scales)
    for p in range(2):
        unpack_late(p)
        wait_main(p)
        unpack(p)
        update(p)
    turn = (iota((share, share), 0) == iota((share, share), 1)).astype(bf16)
    for part in range(2):
        for ex in range(4):
            scales_ref[part, ex] = dot(
                wide_scales[part, ex].astype(bf16), turn, ((0,), (0,))
            ).astype(bf16)


def hand_on_kernel(dir_ref, codes_ref, scales_ref, dir_to, codes_to, scales_to, sem):
    copies = [pltpu.make_async_copy(scales_ref, scales_to, sem.at[12])]
    for ex in range(4):
        copies.append(pltpu.make_async_copy(dir_ref.at[ex], dir_to.at[ex], sem.at[ex]))
        for part in range(2):
            copies.append(
                pltpu.make_async_copy(
                    codes_ref.at[part, ex], codes_to.at[part, ex], sem.at[4 + part * 4 + ex]
                )
            )
    for copy in copies:
        copy.start()
    for copy in copies:
        copy.wait()


def hand_on(*results):
    return tuple(
        pl.pallas_call(
            hand_on_kernel,
            out_shape=tuple(jax.ShapeDtypeStruct(r.shape, r.dtype) for r in results),
            in_specs=[pl.BlockSpec(memory_space=pltpu.VMEM)] * 3,
            out_specs=(pl.BlockSpec(memory_space=pl.ANY),) * 3,
            scratch_shapes=[pltpu.SemaphoreType.DMA((13,))],
            compiler_params=pltpu.CompilerParams(vmem_limit_bytes=8 * 2**20),
            name="hand_on",
        )(*[pltpu.with_memory_space_constraint(r, pltpu.VMEM) for r in results])
    )


def exchange(grad_parts, m_codes, v_codes, m_scale, v_scale, expert_map, slot_expert, slot_row, count, offset):
    slots, width, blocks = m_codes.shape[2], m_codes.shape[3], m_scale.shape[3]
    share = grad_parts.shape[2] // 4
    owned = 4 * share
    vmem = pl.BlockSpec(memory_space=pltpu.VMEM)
    hbm = pl.BlockSpec(memory_space=pl.ANY)
    chunk = 32 * EXTRA
    direction, codes, scales, heavy = pl.pallas_call(
        resume_kernel,
        out_shape=(
            pltpu.VMEM((4, share, width), f32),
            pltpu.VMEM((2, 4, share, width), bf16),
            pltpu.VMEM((2, 4, blocks, share), bf16),
            jax.ShapeDtypeStruct((1,), jnp.int32),
        ),
        in_specs=[hbm] * 3 + [vmem] * 7,
        out_specs=(vmem, vmem, vmem, pl.BlockSpec(memory_space=pltpu.SMEM)),
        scratch_shapes=[
            pltpu.VMEM((slots, 2 * width), bf16),
            pltpu.VMEM((slots, 2 * width), bf16),
            pltpu.VMEM((64 * chunk, 128), f32),
            pltpu.VMEM((64, chunk, 128), bf16),
            pltpu.VMEM((32, chunk, 128), bf16),
            pltpu.VMEM((3, 8, chunk, 128), bf16),
            pltpu.VMEM((7, chunk, 128), bf16),
            pltpu.VMEM((32, chunk, 128), bf16),
            pltpu.VMEM((8, chunk, 128), bf16),
            pltpu.VMEM((2, 64, 16, 512), bf16),
            pltpu.VMEM((2, 64, 16, 512), bf16),
            pltpu.VMEM((64, 384), f32),
            pltpu.VMEM((8, 8, 384), f32),
            pltpu.VMEM((8, 384), f32),
            pltpu.VMEM((8, 384), f32),
            pltpu.VMEM((4, 4, share, width), bf16),
            pltpu.VMEM((4, share, width), f32),
            pltpu.VMEM((4 * owned, 1024), bf16),
            pltpu.VMEM((16 * 32, 128), f32),
            pltpu.VMEM((2, 4, share, 16), f32),
            pltpu.SemaphoreType.DMA((8,)),
            pltpu.SemaphoreType.DMA((2,)),
            pltpu.SemaphoreType.DMA((2,)),
            pltpu.SemaphoreType.DMA((16,)),
            pltpu.SemaphoreType.DMA((16,)),
            pltpu.SemaphoreType.DMA((4,)),
            pltpu.SemaphoreType.DMA((4,)),
            pltpu.SemaphoreType.DMA((2,)),
            pltpu.SemaphoreType.DMA((3,)),
            pltpu.SemaphoreType.DMA((3,)),
            pltpu.SemaphoreType.DMA((7,)),
            pltpu.SemaphoreType.DMA((7,)),
            pltpu.SemaphoreType.REGULAR,
        ],
        compiler_params=pltpu.CompilerParams(
            collective_id=0, has_side_effects=True, vmem_limit_bytes=VMEM_MIB * 2**20
        ),
        name="resume",
    )(
        grad_parts,
        m_codes[0, 0],
        v_codes[0, 0],
        m_scale[0, 0].T,
        v_scale[0, 0].T,
        expert_map.reshape(1, -1),
        slot_expert,
        slot_row,
        count,
        offset,
    )
    return direction, codes, scales, heavy


def per_device(*args):
    direction, codes, scales, heavy = exchange(*args)

    def padded():
        direction, codes, scales = padded_exchange(*args)
        return direction, codes, jnp.swapaxes(scales, 2, 3)

    direction, codes, scales = lax.cond(
        heavy[0] < 2, lambda: hand_on(direction, codes, scales), padded
    )
    return direction, codes, jnp.swapaxes(scales, 2, 3)


def solution(mesh):
    in_specs = (
        P("dp", "expert", None, None),
        P("dp", "expert", None, None),
        P("dp", "expert", None, None),
        P("dp", "expert", None, None),
        P("dp", "expert", None, None),
        P(),
        P("expert", None),
        P("expert", None),
        P("expert", None),
        P("expert", None),
    )
    out_specs = (
        P("expert", "dp", None),
        P(None, "expert", "dp", None),
        P(None, "expert", "dp", None),
    )
    return jax.shard_map(
        per_device, mesh=mesh, in_specs=in_specs, out_specs=out_specs, check_vma=False
    )
```
